32 devices in a mesh: blk: 4 (over x, core), rep: 8 (over z, y).
Axes of the slice: x: 2, y: 2, z: 4, core: 2. Of those that a mesh axis runs over, the one named last changes fastest.
Arguments:
- features: bfloat16 [64, 128, 256], P(('blk', 'rep')), may hold values from -6 to 6
- weight: bfloat16 [256, 256], replicated, may hold values from -0.375 to 0.375
- tile_values: bfloat16 [64, 8, 128, 128], P(('blk', 'rep')), may hold values from -0.1875 to 0.1875
- tile_count: int32 [64], P(('blk', 'rep')), may hold values from 1 to 8, as said below
- tile_cols: int32 [64, 8], P(('blk', 'rep')), may hold values from 0 to 63, as said below
- out_grad: bfloat16 [64, 128, 256], P(('blk', 'rep')), may hold values from -6 to 6
- relu_mask: int32 [64, 128, 256], P(('blk', 'rep')), may hold values 0 or 1
Outputs:
- activated: bfloat16 [64, 128, 256], P(('blk', 'rep'))
- weight_grad: float32 [256, 256], replicated
- in_grad: bfloat16 [64, 128, 256], P(('blk', 'rep'))
The draws below stay inside these ranges and needn't reach their ends.
Inputs may be any that keep to these rules, and one draw needn't show every extreme that they name: `tile_count`: all 2 tile rows of some aligned block of 2 tile rows hold 8 tiles; some tile row holds one. `tile_cols`: tile rows form 8 communities: tile row t belongs to community t // 2 % 8, and every column tile of a tile row lies in its own community; the 8 column tiles of one tile row are distinct; slots not in use hold column tiles too.
All inputs are finite; a program needn't handle non-finite values. No bound on the sum of `relu_mask` on one device may be relied on, other than what follows from the above.
Results may differ from the reference program's by a relative error of at most 0.0049.
Values may be sent and summed in bfloat16 or wider, within the bound.
A program may use at most 64 MiB of HBM per device.

```python
import math
import jax
import jax.numpy as jnp
from jax import lax

F = 256
TILE = 128
TRD = 2
TROWS = 64
COMM = 8
SLOTS = 8
N_REP = 8


def draw_tile_count(key, part):
    block_total = TROWS // TRD
    hot_block = jax.random.randint(jax.random.fold_in(key, 11), (), 0, block_total)
    base_count = jax.random.randint(jax.random.fold_in(key, 12), (TROWS,), 1, 16)
    row_index = jnp.arange(TROWS, dtype=jnp.int32)
    counts = jnp.where(row_index // TRD == hot_block, SLOTS, jnp.minimum(base_count, SLOTS))
    single_row = (hot_block + 1) % block_total * TRD
    counts = jnp.where(row_index == single_row, 1, counts)
    return counts.astype(jnp.int32)


def draw_tile_cols(key, part):
    scores = jax.random.randint(jax.random.fold_in(key, 21), (TROWS, COMM), 0, 65536)
    scores = scores * COMM + jnp.arange(COMM, dtype=jnp.int32)[None, :]
    ranked = jnp.argsort(scores, axis=1, stable=True)[:, :SLOTS].astype(jnp.int32)
    row_index = jnp.arange(TROWS, dtype=jnp.int32)
    community = row_index // TRD % N_REP
    columns = (ranked // TRD * N_REP + community[:, None]) * TRD + ranked % TRD
    return columns.astype(jnp.int32)


def with_ends(entries, own_key, smallest, top_value):
    index_at = [jax.random.randint(jax.random.fold_in(own_key, axis), (), 0, length) for axis, length in enumerate(entries.shape)]
    longest = entries.shape.index(max(entries.shape))
    next_to = index_at[:longest] + [(index_at[longest] + 1) % entries.shape[longest]] + index_at[longest + 1:]
    return entries.at[tuple(index_at)].set(smallest).at[tuple(next_to)].set(top_value)


def level_of(key, extent, shards, low, largest):
    loudness, own = 1.0, jax.random.fold_in(key, 6)
    for position, blocks in shards:
        draws = jnp.exp(jax.random.uniform(jax.random.fold_in(own, position), (blocks,), jnp.float32, low / len(shards), largest / len(shards)))
        loudness = loudness * jnp.repeat(draws, extent[position] // blocks).reshape([-1 if axis == position else 1 for axis in range(len(extent))])
    return loudness


def noise(rng, dims, spread, limit, cuts=(), kind=jnp.bfloat16):
    entries = spread * jax.random.normal(rng, dims, jnp.float32)
    if cuts:
        entries = entries * level_of(rng, dims, cuts, -0.22, 0.18)
    return jnp.clip(entries, -limit, limit).astype(kind)


def setup_inputs(seed: int = 0) -> dict:
    splits = jax.random.split(jax.random.key(seed), 8)
    return {
        "features": noise(splits[0], (TROWS, TILE, F), 1.0, 6.0, ((0, 32),)),
        "weight": noise(splits[1], (F, F), F ** -0.5, 0.375),
        "tile_values": noise(splits[2], (TROWS, SLOTS, TILE, TILE), (TILE * 8) ** -0.5, 0.1875, ((0, 32),)),
        "tile_count": draw_tile_count(jax.random.fold_in(splits[7], 71), 0),
        "tile_cols": draw_tile_cols(jax.random.fold_in(splits[7], 71), 0),
        "out_grad": noise(splits[5], (TROWS, TILE, F), 1.0, 6.0, ((0, 32),)),
        "relu_mask": with_ends((jax.random.randint(splits[6], (TROWS, TILE, F), 0, 2) < 1).astype(jnp.int32), jax.random.fold_in(splits[6], 1), 0, 1),
    }


def reference(features, weight, tile_values, tile_count, tile_cols, out_grad, relu_mask):
    in_use = jnp.arange(SLOTS, dtype=jnp.int32)[None, :] < tile_count[:, None]
    masked = jnp.where(in_use[:, :, None, None], tile_values, jnp.zeros_like(tile_values))

    def forward_row(row_pair):
        tile_block, columns = row_pair
        picked = features[columns].astype(jnp.float32)
        return jnp.einsum('sji,sjf->if', tile_block.astype(jnp.float32), picked)
    aggregate = lax.map(forward_row, (masked, tile_cols)).astype(jnp.bfloat16)
    hidden_flat = aggregate.reshape(-1, F)
    linear = jnp.dot(hidden_flat, weight, preferred_element_type=jnp.float32)
    activated = jnp.maximum(linear, 0.0).astype(jnp.bfloat16).reshape(aggregate.shape)
    grad_flat = out_grad.reshape(-1, F)
    grad_scale = 1.0 / math.sqrt(TROWS * TILE)
    weight_grad = jnp.dot(hidden_flat.T, grad_flat, preferred_element_type=jnp.float32) * grad_scale
    row_grad = jnp.dot(grad_flat, weight.T, preferred_element_type=jnp.float32).astype(jnp.bfloat16)
    row_grad = row_grad.reshape(out_grad.shape)

    def backward_row(accum_grad, row_triple):
        tile_block, columns, grads = row_triple
        contrib = jnp.einsum('sji,if->sjf', tile_block.astype(jnp.float32), grads.astype(jnp.float32))
        return (accum_grad.at[columns].add(contrib), None)
    start_grad = jnp.zeros((TROWS, TILE, F), jnp.float32)
    column_grad, _ = lax.scan(backward_row, start_grad, (masked, tile_cols, row_grad))
    in_grad = (relu_mask.astype(jnp.float32) * column_grad).astype(jnp.bfloat16)
    return (activated, weight_grad, in_grad)
```

```python
import functools
import math

import jax
import jax.numpy as jnp
from jax import lax
from jax.experimental import pallas as pl
from jax.experimental.pallas import tpu as pltpu
from jax.sharding import PartitionSpec as P

MESH = pl.DeviceIdType.MESH
BF16 = jnp.bfloat16
F32 = jnp.float32


def each(count, body):
    if count <= 2:
        for step in range(count):
            body(step)
    else:
        lax.fori_loop(0, count, lambda step, carry: (body(step), carry)[1], 0)


def dot(a, b, contract=((1,), (0,))):
    return lax.dot_general(a, b, (contract, ((), ())), preferred_element_type=F32)


def kernel(dims, *refs):
    blk_size, rep_size, rows_per, slots, tile, width, plane_y, reduce_in = dims
    (count_ref, cols_ref, feat_ref, tv_ref, grad_ref, weight_ref) = refs[:6]
    (act_ref, col_ref, wg_ref) = refs[6:9]
    (tv, grad, weight, feats, mt, rg, own, one_send, one_recv, two_send, two_recv,
     act, col, wg_part, rs_recv, z_buf, wg_full,
     in_sem, out_sem, f_send, f_recv, fwd_send, one_ssem, one_rsem, two_ssem, two_rsem,
     rs_ssem, rs_rsem, z_ssem, z_rsem, ag_ssem, ag_rsem) = refs[9:]
    nodes = rows_per * tile
    chips = blk_size // 2
    z_size = rep_size // plane_y
    plane = blk_size * plane_y
    blk, rep = lax.axis_index("blk"), lax.axis_index("rep")
    chip, core = blk // 2, lax.rem(blk, 2)
    sib = chip * 2 + 1 - core
    my_y, my_z = lax.rem(rep, plane_y), rep // plane_y
    place = my_y * blk_size + blk

    def other_chip(step):
        return lax.rem(chip + 1 + step, chips)

    def plane_id(step):
        there = lax.rem(place + step, plane)
        return there, {"blk": lax.rem(there, blk_size), "rep": my_z * plane_y + there // blk_size}

    def z_id(step):
        there = lax.rem(my_z + step, z_size)
        return there, {"blk": blk, "rep": there * plane_y + my_y}

    loads = [pltpu.make_async_copy(grad_ref, grad, in_sem.at[0]),
             pltpu.make_async_copy(weight_ref, weight, in_sem.at[1])]
    for t in range(rows_per):
        loads.append(pltpu.make_async_copy(tv_ref.at[t], tv.at[t, pl.ds(0, slots)], in_sem.at[2 + t]))
    my_rows = pl.ds(pl.multiple_of(core * nodes, nodes), nodes)
    sib_rows = pl.ds(pl.multiple_of((1 - core) * nodes, nodes), nodes)
    loads.append(pltpu.make_async_copy(feat_ref, feats.at[chip, my_rows], in_sem.at[2 + rows_per]))
    for load in loads:
        load.start()

    barrier = pltpu.get_barrier_semaphore()
    if reduce_in:
        for step in range(1, plane):
            pl.semaphore_signal(barrier, inc=1, device_id=plane_id(step)[1], device_id_type=MESH)
        for step in range(1, z_size):
            pl.semaphore_signal(barrier, inc=1, device_id=z_id(step)[1], device_id_type=MESH)
        greeted = plane - 1 + z_size - 1
    else:
        pl.semaphore_signal(barrier, inc=1, device_id={"blk": sib, "rep": rep}, device_id_type=MESH)
        for step in range(chips - 1):
            pl.semaphore_signal(
                barrier, inc=1, device_id={"blk": other_chip(step) * 2 + core, "rep": rep}, device_id_type=MESH)
        greeted = chips
    loads[0].wait()
    loads[1].wait()
    rg[...] = dot(grad[...], weight[...], ((1,), (1,))).astype(BF16)
    pl.semaphore_wait(barrier, greeted)

    def send_x(step, piece):
        q = other_chip(step)
        rows = pl.ds(pl.multiple_of(core * nodes + piece * tile, tile), tile)
        return pltpu.make_async_remote_copy(
            src_ref=feat_ref.at[pl.ds(piece * tile, tile)], dst_ref=feats.at[chip, rows],
            send_sem=f_send.at[q, piece], recv_sem=f_recv.at[0, chip, piece],
            device_id={"blk": q * 2 + core, "rep": rep}, device_id_type=MESH)

    def came_x(q, piece):
        rows = pl.ds(pl.multiple_of(core * nodes + piece * tile, tile), tile)
        return pltpu.make_async_remote_copy(
            src_ref=feat_ref.at[pl.ds(piece * tile, tile)], dst_ref=feats.at[q, rows],
            send_sem=f_send.at[q, piece], recv_sem=f_recv.at[0, q, piece],
            device_id={"blk": q * 2 + core, "rep": rep}, device_id_type=MESH)

    def pass_on(q, piece):
        rows = pl.ds(pl.multiple_of(core * nodes + piece * tile, tile), tile)
        return pltpu.make_async_remote_copy(
            src_ref=feats.at[q, rows], dst_ref=feats.at[q, rows],
            send_sem=fwd_send.at[q, piece], recv_sem=f_recv.at[1, q, piece],
            device_id={"blk": sib, "rep": rep}, device_id_type=MESH)

    def passed(q, piece):
        rows = pl.ds(pl.multiple_of((1 - core) * nodes + piece * tile, tile), tile)
        return pltpu.make_async_remote_copy(
            src_ref=feats.at[q, rows], dst_ref=feats.at[q, rows],
            send_sem=fwd_send.at[q, piece], recv_sem=f_recv.at[1, q, piece],
            device_id={"blk": sib, "rep": rep}, device_id_type=MESH)

    for piece in range(rows_per):
        each(chips - 1, lambda step: send_x(step, piece).start())
    loads[-1].wait()
    for piece in range(rows_per):
        pass_on(chip, piece).start()

    for t in range(rows_per):
        loads[2 + t].wait()
        tv[t, slots] = jnp.zeros((tile, tile), BF16)

    def block_of(q, c):
        member = q * 2 + c
        bands = []
        for r in range(rows_per):
            column = (member * rep_size + rep) * rows_per + r
            pieces = []
            for t in range(rows_per):
                slot = jnp.int32(slots)
                for s in range(slots):
                    hit = jnp.logical_and(cols_ref[t, s] == column, s < count_ref[t])
                    slot = jnp.where(hit, jnp.int32(s), slot)
                pieces.append(tv[t, slot])
            bands.append(jnp.concatenate(pieces, axis=1))
        return jnp.concatenate(bands, axis=0)

    def one_copy(q):
        return pltpu.make_async_remote_copy(
            src_ref=one_send.at[q], dst_ref=one_recv.at[q],
            send_sem=one_ssem.at[q], recv_sem=one_rsem.at[q],
            device_id={"blk": sib, "rep": rep}, device_id_type=MESH)

    def two_copy(q, slot):
        return pltpu.make_async_remote_copy(
            src_ref=two_send.at[q], dst_ref=two_recv.at[slot],
            send_sem=two_ssem.at[q], recv_sem=two_rsem.at[slot],
            device_id={"blk": q * 2 + core, "rep": rep}, device_id_type=MESH)

    def for_sibling(step):
        q = other_chip(step)
        block = block_of(q, 1 - core)
        one_send[q] = dot(block, rg[...]).astype(BF16)
        one_copy(q).start()
        mt[q, :, sib_rows] = block.T

    def for_core(step):
        q = other_chip(step)
        block = block_of(q, core)
        own[q] = dot(block, rg[...])
        mt[q, :, my_rows] = block.T

    each(chips, for_sibling)
    each(chips, for_core)

    def second(step):
        q = other_chip(step)
        one_copy(q).wait_recv()
        two_send[q] = (own[q] + one_recv[q].astype(F32)).astype(BF16)
        two_copy(q, chip).start()

    def hand_on(step):
        q = other_chip(step)
        for piece in range(rows_per):
            came_x(q, piece).wait_recv()
            pass_on(q, piece).start()

    each(chips - 1, second)
    each(chips - 1, hand_on)

    for piece in range(rows_per):
        passed(chip, piece).wait_recv()
    own_part = dot(mt[chip], feats[chip])
    act[...] = own_part

    def forward(step):
        q = other_chip(step)
        for piece in range(rows_per):
            passed(q, piece).wait_recv()
        act[...] += dot(mt[q], feats[q])

    each(chips - 1, forward)
    hidden = act[...].astype(BF16)
    term = dot(hidden, grad[...], ((0,), (0,)))

    if reduce_in:
        share = width // plane
        wg_part[...] = term.astype(BF16)

        def rs_copy(step):
            there, device = plane_id(step)
            return pltpu.make_async_remote_copy(
                src_ref=wg_part.at[pl.ds(pl.multiple_of(there * share, share), share)],
                dst_ref=rs_recv.at[step - 1],
                send_sem=rs_ssem.at[step - 1], recv_sem=rs_rsem.at[step - 1],
                device_id=device, device_id_type=MESH)

        for step in range(1, plane):
            rs_copy(step).start()
    else:
        wg_ref[...] = term

    act_ref[...] = dot(hidden, weight[...]).astype(BF16)
    one_copy(chip).wait_recv()
    col[...] = own[chip] + one_recv[chip].astype(F32)

    def gathered(step):
        q = other_chip(step)
        two_copy(q, q).wait_recv()
        col[...] += two_recv[q].astype(F32)

    each(chips - 1, gathered)
    col_ref[...] = col[...].astype(BF16)

    if reduce_in:
        my_share = pl.ds(pl.multiple_of(place * share, share), share)
        total = wg_part[my_share].astype(F32)
        for step in range(1, plane):
            rs_copy(step).wait_recv()
            total = total + rs_recv[step - 1].astype(F32)
        z_buf[my_z] = total.astype(BF16)

        def z_copy(step, slot):
            return pltpu.make_async_remote_copy(
                src_ref=z_buf.at[my_z], dst_ref=z_buf.at[slot],
                send_sem=z_ssem.at[step - 1], recv_sem=z_rsem.at[slot],
                device_id=z_id(step)[1], device_id_type=MESH)

        for step in range(1, z_size):
            z_copy(step, my_z).start()
        for step in range(1, z_size):
            z_copy(step, z_id(step)[0]).wait_recv()
        total = z_buf[0].astype(F32)
        for z in range(1, z_size):
            total = total + z_buf[z].astype(F32)
        scale = 1.0 / math.sqrt(nodes * blk_size * rep_size)
        wg_full[my_share] = (total * scale).astype(BF16)

        def ag_copy(step, owner):
            rows = pl.ds(pl.multiple_of(owner * share, share), share)
            return pltpu.make_async_remote_copy(
                src_ref=wg_full.at[rows], dst_ref=wg_full.at[rows],
                send_sem=ag_ssem.at[step - 1], recv_sem=ag_rsem.at[step - 1],
                device_id=plane_id(step)[1], device_id_type=MESH)

        for step in range(1, plane):
            ag_copy(step, place).start()
        for step in range(1, plane):
            ag_copy(step, lax.rem(place + plane - step, plane)).wait_recv()
        wg_ref[...] = wg_full[...].astype(F32)

    for piece in range(rows_per):
        each(chips - 1, lambda step: send_x(step, piece).wait_send())
        each(chips, lambda step: pass_on(other_chip(step), piece).wait_send())
    each(chips, lambda step: one_copy(other_chip(step)).wait_send())
    each(chips - 1, lambda step: two_copy(other_chip(step), chip).wait_send())
    if reduce_in:
        for step in range(1, plane):
            rs_copy(step).wait_send()
            ag_copy(step, place).wait_send()
        for step in range(1, z_size):
            z_copy(step, my_z).wait_send()


def per_device(features, weight, tile_values, tile_count, tile_cols, out_grad, relu_mask):
    rows_per, slots, tile = tile_values.shape[:3]
    width = features.shape[2]
    nodes = rows_per * tile
    blk_size, rep_size = lax.axis_size("blk"), lax.axis_size("rep")
    chips = blk_size // 2
    plane_y = 2
    z_size = rep_size // plane_y
    plane = blk_size * plane_y
    reduce_in = width % (plane * 16) == 0 and z_size <= 8
    share = width // plane if reduce_in else 16
    block = (nodes, width)
    dma = pltpu.SemaphoreType.DMA
    vmem = pltpu.VMEM
    scratch = [
        vmem((rows_per, slots + 1, tile, tile), BF16),
        vmem(block, BF16),
        vmem((width, width), BF16),
        vmem((chips, 2 * nodes, width), BF16),
        vmem((chips, nodes, 2 * nodes), BF16),
        vmem(block, BF16),
        vmem((chips,) + block, F32),
        vmem((chips,) + block, BF16),
        vmem((chips,) + block, BF16),
        vmem((chips,) + block, BF16),
        vmem((chips,) + block, BF16),
        vmem(block, F32),
        vmem(block, F32),
        vmem((width, width), BF16),
        vmem((plane - 1, share, width), BF16),
        vmem((z_size, share, width), BF16),
        vmem((width, width), BF16),
        dma((3 + rows_per,)), dma((2,)),
        dma((chips, rows_per)), dma((2, chips, rows_per)), dma((chips, rows_per)),
        dma((chips,)), dma((chips,)), dma((chips,)), dma((chips,)),
        dma((plane - 1,)), dma((plane - 1,)), dma((z_size,)), dma((z_size,)),
        dma((plane - 1,)), dma((plane - 1,)),
    ]
    smem = pl.BlockSpec(memory_space=pltpu.SMEM)
    hbm = pl.BlockSpec(memory_space=pl.ANY)
    whole = pl.BlockSpec(memory_space=pltpu.VMEM)
    dims = (blk_size, rep_size, rows_per, slots, tile, width, plane_y, reduce_in)
    linear, column, weight_term = pl.pallas_call(
        functools.partial(kernel, dims),
        out_shape=(
            jax.ShapeDtypeStruct(block, BF16),
            jax.ShapeDtypeStruct(block, BF16),
            jax.ShapeDtypeStruct((width, width), F32),
        ),
        in_specs=[smem, smem, hbm, hbm, hbm, hbm],
        out_specs=(whole, whole, whole),
        scratch_shapes=scratch,
        compiler_params=pltpu.CompilerParams(
            collective_id=0, has_side_effects=True, vmem_limit_bytes=32 * 1024 * 1024
        ),
        name="layer",
    )(tile_count, tile_cols, features.reshape(block), tile_values, out_grad.reshape(block), weight)
    activated = jnp.maximum(linear, 0).reshape(features.shape)
    in_grad = jnp.where(relu_mask != 0, column.reshape(features.shape), jnp.zeros((), BF16))
    if not reduce_in:
        scale = 1.0 / math.sqrt(nodes * blk_size * rep_size)
        weight_term = lax.psum(weight_term, ("blk", "rep")) * scale
    return (activated, weight_term, in_grad)


def solution(mesh):
    placed = (
        P(("blk", "rep"), None, None),
        P(),
        P(("blk", "rep"), None, None, None),
        P(("blk", "rep")),
        P(("blk", "rep"), None),
        P(("blk", "rep"), None, None),
        P(("blk", "rep"), None, None),
    )
    return jax.shard_map(
        per_device,
        mesh=mesh,
        in_specs=placed,
        out_specs=(P(("blk", "rep"), None, None), P(), P(("blk", "rep"), None, None)),
        check_vma=False,
    )
```

```python
import functools
import math

import jax
import jax.numpy as jnp
from jax import lax
from jax.experimental import pallas as pl
from jax.experimental.pallas import tpu as pltpu
from jax.sharding import PartitionSpec as P

MESH = pl.DeviceIdType.MESH
BF16 = jnp.bfloat16
F32 = jnp.float32


def each(count, body):
    if count <= 2:
        for step in range(count):
            body(step)
    else:
        lax.fori_loop(0, count, lambda step, carry: (body(step), carry)[1], 0)


def dot(a, b, contract=((1,), (0,))):
    return lax.dot_general(a, b, (contract, ((), ())), preferred_element_type=F32)


def kernel(dims, *refs):
    blk_size, rep_size, rows_per, slots, tile, width, plane_y, reduce_in = dims
    (count_hbm, cols_hbm, feat_ref, tv_ref, grad_ref, weight_ref, mask_ref) = refs[:7]
    (act_ref, col_ref, wg_ref) = refs[7:10]
    (count_ref, cols_ref, mask, tv, grad, weight, feats, mt, rg, own, one_send, one_recv, two_send, two_recv,
     act, col, wg_part, rs_recv, z_buf, wg_full,
     in_sem, f_send, f_recv, fwd_send, one_ssem, one_rsem, two_ssem, two_rsem,
     rs_ssem, rs_rsem, z_ssem, z_rsem, ag_ssem, ag_rsem) = refs[10:]
    nodes = rows_per * tile
    chips = blk_size // 2
    z_size = rep_size // plane_y
    plane = blk_size * plane_y
    blk, rep = lax.axis_index("blk"), lax.axis_index("rep")
    chip, core = blk // 2, lax.rem(blk, 2)
    sib = chip * 2 + 1 - core
    my_y, my_z = lax.rem(rep, plane_y), rep // plane_y
    place = my_y * blk_size + blk

    def other_chip(step):
        return lax.rem(chip + 1 + step, chips)

    def plane_id(step):
        there = lax.rem(place + step, plane)
        return there, {"blk": lax.rem(there, blk_size), "rep": my_z * plane_y + there // blk_size}

    def z_id(step):
        there = lax.rem(my_z + step, z_size)
        return there, {"blk": blk, "rep": there * plane_y + my_y}

    loads = [pltpu.make_async_copy(grad_ref, grad, in_sem.at[0]),
             pltpu.make_async_copy(weight_ref, weight, in_sem.at[1])]
    for t in range(rows_per):
        loads.append(pltpu.make_async_copy(tv_ref.at[t], tv.at[t, pl.ds(0, slots)], in_sem.at[2 + t]))
    my_rows = pl.ds(pl.multiple_of(core * nodes, nodes), nodes)
    sib_rows = pl.ds(pl.multiple_of((1 - core) * nodes, nodes), nodes)
    loads.append(pltpu.make_async_copy(feat_ref, feats.at[chip, my_rows], in_sem.at[2 + rows_per]))
    loads.append(pltpu.make_async_copy(count_hbm, count_ref, in_sem.at[3 + rows_per]))
    loads.append(pltpu.make_async_copy(cols_hbm, cols_ref, in_sem.at[4 + rows_per]))
    loads.append(pltpu.make_async_copy(mask_ref, mask, in_sem.at[5 + rows_per]))
    for load in loads:
        load.start()

    barrier = pltpu.get_barrier_semaphore()
    if reduce_in:
        for step in range(1, plane):
            pl.semaphore_signal(barrier, inc=1, device_id=plane_id(step)[1], device_id_type=MESH)
        for step in range(1, z_size):
            pl.semaphore_signal(barrier, inc=1, device_id=z_id(step)[1], device_id_type=MESH)
        greeted = plane - 1 + z_size - 1
    else:
        pl.semaphore_signal(barrier, inc=1, device_id={"blk": sib, "rep": rep}, device_id_type=MESH)
        for step in range(chips - 1):
            pl.semaphore_signal(
                barrier, inc=1, device_id={"blk": other_chip(step) * 2 + core, "rep": rep}, device_id_type=MESH)
        greeted = chips
    loads[0].wait()
    loads[1].wait()
    rg[...] = dot(grad[...], weight[...], ((1,), (1,))).astype(BF16)
    pl.semaphore_wait(barrier, greeted)

    def send_x(step, piece):
        q = other_chip(step)
        rows = pl.ds(pl.multiple_of(core * nodes + piece * tile, tile), tile)
        return pltpu.make_async_remote_copy(
            src_ref=feat_ref.at[pl.ds(piece * tile, tile)], dst_ref=feats.at[chip, rows],
            send_sem=f_send.at[q, piece], recv_sem=f_recv.at[0, chip, piece],
            device_id={"blk": q * 2 + core, "rep": rep}, device_id_type=MESH)

    def came_x(q, piece):
        rows = pl.ds(pl.multiple_of(core * nodes + piece * tile, tile), tile)
        return pltpu.make_async_remote_copy(
            src_ref=feat_ref.at[pl.ds(piece * tile, tile)], dst_ref=feats.at[q, rows],
            send_sem=f_send.at[q, piece], recv_sem=f_recv.at[0, q, piece],
            device_id={"blk": q * 2 + core, "rep": rep}, device_id_type=MESH)

    def pass_on(q, piece):
        rows = pl.ds(pl.multiple_of(core * nodes + piece * tile, tile), tile)
        return pltpu.make_async_remote_copy(
            src_ref=feats.at[q, rows], dst_ref=feats.at[q, rows],
            send_sem=fwd_send.at[q, piece], recv_sem=f_recv.at[1, q, piece],
            device_id={"blk": sib, "rep": rep}, device_id_type=MESH)

    def passed(q, piece):
        rows = pl.ds(pl.multiple_of((1 - core) * nodes + piece * tile, tile), tile)
        return pltpu.make_async_remote_copy(
            src_ref=feats.at[q, rows], dst_ref=feats.at[q, rows],
            send_sem=fwd_send.at[q, piece], recv_sem=f_recv.at[1, q, piece],
            device_id={"blk": sib, "rep": rep}, device_id_type=MESH)

    for piece in range(rows_per):
        each(chips - 1, lambda step: send_x(step, piece).start())
    loads[2 + rows_per].wait()
    for piece in range(rows_per):
        pass_on(chip, piece).start()

    loads[3 + rows_per].wait()
    loads[4 + rows_per].wait()
    for t in range(rows_per):
        loads[2 + t].wait()
        tv[t, slots] = jnp.zeros((tile, tile), BF16)

    def block_of(q, c):
        member = q * 2 + c
        bands = []
        for r in range(rows_per):
            column = (member * rep_size + rep) * rows_per + r
            pieces = []
            for t in range(rows_per):
                slot = jnp.int32(slots)
                for s in range(slots):
                    hit = jnp.logical_and(cols_ref[t, s] == column, s < count_ref[t])
                    slot = jnp.where(hit, jnp.int32(s), slot)
                pieces.append(tv[t, slot])
            bands.append(jnp.concatenate(pieces, axis=1))
        return jnp.concatenate(bands, axis=0)

    def one_copy(q):
        return pltpu.make_async_remote_copy(
            src_ref=one_send.at[q], dst_ref=one_recv.at[q],
            send_sem=one_ssem.at[q], recv_sem=one_rsem.at[q],
            device_id={"blk": sib, "rep": rep}, device_id_type=MESH)

    def two_copy(q, slot):
        return pltpu.make_async_remote_copy(
            src_ref=two_send.at[q], dst_ref=two_recv.at[slot],
            send_sem=two_ssem.at[q], recv_sem=two_rsem.at[slot],
            device_id={"blk": q * 2 + core, "rep": rep}, device_id_type=MESH)

    def for_sibling(step):
        q = other_chip(step)
        block = block_of(q, 1 - core)
        one_send[q] = dot(block, rg[...]).astype(BF16)
        one_copy(q).start()
        mt[q, :, sib_rows] = block.T

    def for_core(step):
        q = other_chip(step)
        block = block_of(q, core)
        own[q] = dot(block, rg[...])
        mt[q, :, my_rows] = block.T

    each(chips, for_sibling)
    each(chips, for_core)

    def second(step):
        q = other_chip(step)
        one_copy(q).wait_recv()
        two_send[q] = (own[q] + one_recv[q].astype(F32)).astype(BF16)
        two_copy(q, chip).start()

    def hand_on(step):
        q = other_chip(step)
        for piece in range(rows_per):
            came_x(q, piece).wait_recv()
            pass_on(q, piece).start()

    each(chips - 1, hand_on)

    for piece in range(rows_per):
        passed(chip, piece).wait_recv()
    own_part = dot(mt[chip], feats[chip])
    act[...] = own_part

    def forward(step):
        q = other_chip(step)
        for piece in range(rows_per):
            passed(q, piece).wait_recv()
        act[...] += dot(mt[q], feats[q])

    each(chips - 1, forward)
    hidden = act[...].astype(BF16)
    term = dot(hidden, grad[...], ((0,), (0,)))

    if reduce_in:
        share = width // plane
        wg_part[...] = term.astype(BF16)

        def rs_copy(step):
            there, device = plane_id(step)
            return pltpu.make_async_remote_copy(
                src_ref=wg_part.at[pl.ds(pl.multiple_of(there * share, share), share)],
                dst_ref=rs_recv.at[step - 1],
                send_sem=rs_ssem.at[step - 1], recv_sem=rs_rsem.at[step - 1],
                device_id=device, device_id_type=MESH)

        for step in range(1, plane):
            rs_copy(step).start()
    else:
        wg_ref[...] = term
    each(chips - 1, second)

    act_ref[...] = jnp.maximum(dot(hidden, weight[...]), 0.0).astype(BF16)
    one_copy(chip).wait_recv()
    col[...] = own[chip] + one_recv[chip].astype(F32)

    def gathered(step):
        q = other_chip(step)
        two_copy(q, q).wait_recv()
        col[...] += two_recv[q].astype(F32)

    each(chips - 1, gathered)
    loads[5 + rows_per].wait()
    col_ref[...] = (mask[...].astype(F32) * col[...]).astype(BF16)

    if reduce_in:
        my_share = pl.ds(pl.multiple_of(place * share, share), share)
        total = wg_part[my_share].astype(F32)
        for step in range(1, plane):
            rs_copy(step).wait_recv()
            total = total + rs_recv[step - 1].astype(F32)
        z_buf[my_z] = total.astype(BF16)

        def z_copy(step, slot):
            return pltpu.make_async_remote_copy(
                src_ref=z_buf.at[my_z], dst_ref=z_buf.at[slot],
                send_sem=z_ssem.at[step - 1], recv_sem=z_rsem.at[slot],
                device_id=z_id(step)[1], device_id_type=MESH)

        for step in range(1, z_size):
            z_copy(step, my_z).start()
        for step in range(1, z_size):
            z_copy(step, z_id(step)[0]).wait_recv()
        total = z_buf[0].astype(F32)
        for z in range(1, z_size):
            total = total + z_buf[z].astype(F32)
        scale = 1.0 / math.sqrt(nodes * blk_size * rep_size)
        wg_full[my_share] = (total * scale).astype(BF16)

        def ag_copy(step, owner):
            rows = pl.ds(pl.multiple_of(owner * share, share), share)
            return pltpu.make_async_remote_copy(
                src_ref=wg_full.at[rows], dst_ref=wg_full.at[rows],
                send_sem=ag_ssem.at[step - 1], recv_sem=ag_rsem.at[step - 1],
                device_id=plane_id(step)[1], device_id_type=MESH)

        for step in range(1, plane):
            ag_copy(step, place).start()
        for step in range(1, plane):
            ag_copy(step, lax.rem(place + plane - step, plane)).wait_recv()
        wg_ref[...] = wg_full[...].astype(F32)

    for piece in range(rows_per):
        each(chips - 1, lambda step: send_x(step, piece).wait_send())
        each(chips, lambda step: pass_on(other_chip(step), piece).wait_send())
    each(chips, lambda step: one_copy(other_chip(step)).wait_send())
    each(chips - 1, lambda step: two_copy(other_chip(step), chip).wait_send())
    if reduce_in:
        for step in range(1, plane):
            rs_copy(step).wait_send()
            ag_copy(step, place).wait_send()
        for step in range(1, z_size):
            z_copy(step, my_z).wait_send()


def write_out(a_ref, b_ref, c_ref, a_out, b_out, c_out, sem):
    copies = [pltpu.make_async_copy(src, dst, sem.at[i])
              for i, (src, dst) in enumerate(((a_ref, a_out), (b_ref, b_out), (c_ref, c_out)))]
    for copy in copies:
        copy.start()
    for copy in copies:
        copy.wait()


def per_device(features, weight, tile_values, tile_count, tile_cols, out_grad, relu_mask):
    rows_per, slots, tile = tile_values.shape[:3]
    width = features.shape[2]
    nodes = rows_per * tile
    blk_size, rep_size = lax.axis_size("blk"), lax.axis_size("rep")
    chips = blk_size // 2
    plane_y = 2
    z_size = rep_size // plane_y
    plane = blk_size * plane_y
    reduce_in = width % (plane * 16) == 0 and z_size <= 8
    share = width // plane if reduce_in else 16
    block = (nodes, width)
    dma = pltpu.SemaphoreType.DMA
    vmem = pltpu.VMEM
    scratch = [
        pltpu.SMEM((rows_per,), jnp.int32),
        pltpu.SMEM((rows_per, slots), jnp.int32),
        vmem(block, jnp.int32),
        vmem((rows_per, slots + 1, tile, tile), BF16),
        vmem(block, BF16),
        vmem((width, width), BF16),
        vmem((chips, 2 * nodes, width), BF16),
        vmem((chips, nodes, 2 * nodes), BF16),
        vmem(block, BF16),
        vmem((chips,) + block, F32),
        vmem((chips,) + block, BF16),
        vmem((chips,) + block, BF16),
        vmem((chips,) + block, BF16),
        vmem((chips,) + block, BF16),
        vmem(block, F32),
        vmem(block, F32),
        vmem((width, width), BF16),
        vmem((plane - 1, share, width), BF16),
        vmem((z_size, share, width), BF16),
        vmem((width, width), BF16),
        dma((6 + rows_per,)),
        dma((chips, rows_per)), dma((2, chips, rows_per)), dma((chips, rows_per)),
        dma((chips,)), dma((chips,)), dma((chips,)), dma((chips,)),
        dma((plane - 1,)), dma((plane - 1,)), dma((z_size,)), dma((z_size,)),
        dma((plane - 1,)), dma((plane - 1,)),
    ]
    hbm = pl.BlockSpec(memory_space=pltpu.HBM)
    whole = pl.BlockSpec(memory_space=pltpu.VMEM)
    dims = (blk_size, rep_size, rows_per, slots, tile, width, plane_y, reduce_in)
    results = pl.pallas_call(
        functools.partial(kernel, dims),
        out_shape=(
            jax.ShapeDtypeStruct(block, BF16),
            jax.ShapeDtypeStruct(block, BF16),
            jax.ShapeDtypeStruct((width, width), F32),
        ),
        in_specs=[hbm] * 7,
        out_specs=(whole, whole, whole),
        scratch_shapes=scratch,
        compiler_params=pltpu.CompilerParams(
            collective_id=0, has_side_effects=True, vmem_limit_bytes=32 * 1024 * 1024
        ),
        name="layer",
    )(*[pltpu.with_memory_space_constraint(x, pltpu.HBM) for x in (
        tile_count, tile_cols, features.reshape(block), tile_values, out_grad.reshape(block), weight,
        relu_mask.reshape(block))])
    activated, in_grad, weight_term = pl.pallas_call(
        write_out,
        out_shape=tuple(jax.ShapeDtypeStruct(r.shape, r.dtype) for r in results),
        in_specs=[whole] * 3,
        out_specs=(hbm, hbm, hbm),
        scratch_shapes=[dma((3,))],
        name="write_out",
    )(*results)
    activated, in_grad = activated.reshape(features.shape), in_grad.reshape(features.shape)
    if not reduce_in:
        scale = 1.0 / math.sqrt(nodes * blk_size * rep_size)
        weight_term = lax.psum(weight_term, ("blk", "rep")) * scale
    return (activated, weight_term, in_grad)


def solution(mesh):
    placed = (
        P(("blk", "rep"), None, None),
        P(),
        P(("blk", "rep"), None, None, None),
        P(("blk", "rep")),
        P(("blk", "rep"), None),
        P(("blk", "rep"), None, None),
        P(("blk", "rep"), None, None),
    )
    return jax.shard_map(
        per_device,
        mesh=mesh,
        in_specs=placed,
        out_specs=(P(("blk", "rep"), None, None), P(), P(("blk", "rep"), None, None)),
        check_vma=False,
    )
```

```python
import functools
import math

import jax
import jax.numpy as jnp
from jax import lax
from jax.experimental import pallas as pl
from jax.experimental.pallas import tpu as pltpu
from jax.sharding import PartitionSpec as P

MESH = pl.DeviceIdType.MESH
BF16 = jnp.bfloat16
F32 = jnp.float32


def each(count, body):
    if count <= 2:
        for step in range(count):
            body(step)
    else:
        lax.fori_loop(0, count, lambda step, carry: (body(step), carry)[1], 0)


def dot(a, b, contract=((1,), (0,))):
    return lax.dot_general(a, b, (contract, ((), ())), preferred_element_type=F32)


def kernel(dims, *refs):
    blk_size, rep_size, rows_per, slots, tile, width, plane_y, reduce_in = dims
    (count_hbm, cols_hbm, feat_ref, tv_ref, grad_ref, weight_ref, mask_ref) = refs[:7]
    (act_ref, col_ref, wg_ref) = refs[7:10]
    (count_ref, cols_ref, mask, tv, grad, weight, feats, dense, own, one_send, one_recv, two_send, two_recv,
     act, col, term, wg_part, rs_recv, z_buf, wg_full,
     in_sem, f_send, f_recv, fwd_send, one_ssem, one_rsem, two_ssem, two_rsem,
     rs_ssem, rs_rsem, z_ssem, z_rsem, ag_ssem, ag_rsem) = refs[10:]
    nodes = rows_per * tile
    chips = blk_size // 2
    z_size = rep_size // plane_y
    plane = blk_size * plane_y
    blk, rep = lax.axis_index("blk"), lax.axis_index("rep")
    chip, core = blk // 2, lax.rem(blk, 2)
    sib = chip * 2 + 1 - core
    my_y, my_z = lax.rem(rep, plane_y), rep // plane_y
    place = my_y * blk_size + blk

    def other_chip(step):
        return lax.rem(chip + 1 + step, chips)

    def plane_id(step):
        there = lax.rem(place + step, plane)
        return there, {"blk": lax.rem(there, blk_size), "rep": my_z * plane_y + there // blk_size}

    def z_id(step):
        there = lax.rem(my_z + step, z_size)
        return there, {"blk": blk, "rep": there * plane_y + my_y}

    barrier = pltpu.get_barrier_semaphore()
    if reduce_in:
        for step in range(1, plane):
            pl.semaphore_signal(barrier, inc=1, device_id=plane_id(step)[1], device_id_type=MESH)
        for step in range(1, z_size):
            pl.semaphore_signal(barrier, inc=1, device_id=z_id(step)[1], device_id_type=MESH)
        greeted = plane - 1 + z_size - 1
    else:
        pl.semaphore_signal(barrier, inc=1, device_id={"blk": sib, "rep": rep}, device_id_type=MESH)
        for step in range(chips - 1):
            pl.semaphore_signal(
                barrier, inc=1, device_id={"blk": other_chip(step) * 2 + core, "rep": rep}, device_id_type=MESH)
        greeted = chips

    loads = [pltpu.make_async_copy(grad_ref, grad, in_sem.at[0]),
             pltpu.make_async_copy(weight_ref, weight, in_sem.at[1])]
    for t in range(rows_per):
        loads.append(pltpu.make_async_copy(tv_ref.at[t], tv.at[t, pl.ds(0, slots)], in_sem.at[2 + t]))
    my_rows = pl.ds(pl.multiple_of(core * nodes, nodes), nodes)
    sib_rows = pl.ds(pl.multiple_of((1 - core) * nodes, nodes), nodes)
    loads.append(pltpu.make_async_copy(feat_ref, feats.at[chip, my_rows], in_sem.at[2 + rows_per]))
    loads.append(pltpu.make_async_copy(count_hbm, count_ref, in_sem.at[3 + rows_per]))
    loads.append(pltpu.make_async_copy(cols_hbm, cols_ref, in_sem.at[4 + rows_per]))
    loads.append(pltpu.make_async_copy(mask_ref, mask, in_sem.at[5 + rows_per]))
    for load in loads:
        load.start()
    pl.semaphore_wait(barrier, greeted)

    def send_x(step, piece):
        q = other_chip(step)
        rows = pl.ds(pl.multiple_of(core * nodes + piece * tile, tile), tile)
        return pltpu.make_async_remote_copy(
            src_ref=feat_ref.at[pl.ds(piece * tile, tile)], dst_ref=feats.at[chip, rows],
            send_sem=f_send.at[q, piece], recv_sem=f_recv.at[0, chip, piece],
            device_id={"blk": q * 2 + core, "rep": rep}, device_id_type=MESH)

    def came_x(q, piece):
        rows = pl.ds(pl.multiple_of(core * nodes + piece * tile, tile), tile)
        return pltpu.make_async_remote_copy(
            src_ref=feat_ref.at[pl.ds(piece * tile, tile)], dst_ref=feats.at[q, rows],
            send_sem=f_send.at[q, piece], recv_sem=f_recv.at[0, q, piece],
            device_id={"blk": q * 2 + core, "rep": rep}, device_id_type=MESH)

    def pass_on(q, piece):
        rows = pl.ds(pl.multiple_of(core * nodes + piece * tile, tile), tile)
        return pltpu.make_async_remote_copy(
            src_ref=feats.at[q, rows], dst_ref=feats.at[q, rows],
            send_sem=fwd_send.at[q, piece], recv_sem=f_recv.at[1, q, piece],
            device_id={"blk": sib, "rep": rep}, device_id_type=MESH)

    def passed(q, piece):
        rows = pl.ds(pl.multiple_of((1 - core) * nodes + piece * tile, tile), tile)
        return pltpu.make_async_remote_copy(
            src_ref=feats.at[q, rows], dst_ref=feats.at[q, rows],
            send_sem=fwd_send.at[q, piece], recv_sem=f_recv.at[1, q, piece],
            device_id={"blk": sib, "rep": rep}, device_id_type=MESH)

    for piece in range(rows_per):
        each(chips - 1, lambda step: send_x(step, piece).start())
    loads[2 + rows_per].wait()
    for piece in range(rows_per):
        pass_on(chip, piece).start()

    loads[3 + rows_per].wait()
    loads[4 + rows_per].wait()
    loads[0].wait()
    for t in range(rows_per):
        loads[2 + t].wait()
        tv[t, slots] = jnp.zeros((tile, tile), BF16)

    used = [[jnp.where(s < count_ref[t], cols_ref[t, s], -1) for s in range(slots)] for t in range(rows_per)]

    def block_of(q, c):
        member = q * 2 + c
        bands = []
        for r in range(rows_per):
            column = (member * rep_size + rep) * rows_per + r
            pieces = []
            for t in range(rows_per):
                slot = jnp.int32(slots)
                for s in range(slots):
                    slot = jnp.where(used[t][s] == column, jnp.int32(s), slot)
                pieces.append(tv[t, slot])
            bands.append(jnp.concatenate(pieces, axis=1))
        return jnp.concatenate(bands, axis=0)

    def one_copy(q):
        return pltpu.make_async_remote_copy(
            src_ref=one_send.at[q], dst_ref=one_recv.at[q],
            send_sem=one_ssem.at[q], recv_sem=one_rsem.at[q],
            device_id={"blk": sib, "rep": rep}, device_id_type=MESH)

    def two_copy(q, slot):
        return pltpu.make_async_remote_copy(
            src_ref=two_send.at[q], dst_ref=two_recv.at[slot],
            send_sem=two_ssem.at[q], recv_sem=two_rsem.at[slot],
            device_id={"blk": q * 2 + core, "rep": rep}, device_id_type=MESH)

    def for_sibling(step):
        q = other_chip(step)
        block = block_of(q, 1 - core)
        one_send[q] = dot(block, grad[...]).astype(BF16)
        one_copy(q).start()
        dense[q, sib_rows] = block

    def for_core(step):
        q = other_chip(step)
        block = block_of(q, core)
        own[q] = dot(block, grad[...])
        dense[q, my_rows] = block

    def pair(step):
        q = other_chip(step)
        one_copy(q).wait_recv()
        total = own[q] + one_recv[q].astype(F32)
        own[q] = total
        two_send[q] = total.astype(BF16)

    each(chips, for_sibling)
    each(chips, for_core)
    each(chips, pair)

    term[...] = dot(feats[chip, my_rows], two_send[chip], ((0,), (0,)))

    def arrive(step):
        q = other_chip(step)
        for piece in range(rows_per):
            came_x(q, piece).wait_recv()
            pass_on(q, piece).start()
        term[...] += dot(feats[q, my_rows], two_send[q], ((0,), (0,)))

    each(chips - 1, arrive)

    def forward():
        for piece in range(rows_per):
            passed(chip, piece).wait_recv()
        act[...] = dot(dense[chip], feats[chip], ((0,), (0,)))

        def from_chip(step):
            q = other_chip(step)
            for piece in range(rows_per):
                passed(q, piece).wait_recv()
            act[...] += dot(dense[q], feats[q], ((0,), (0,)))

        each(chips - 1, from_chip)

    def activate():
        loads[1].wait()
        act_ref[...] = jnp.maximum(dot(act[...].astype(BF16), weight[...]), 0.0).astype(BF16)

    def columns():
        col[...] = own[chip]

        def from_chip(step):
            q = other_chip(step)
            two_copy(q, q).wait_recv()
            col[...] += two_recv[q].astype(F32)

        each(chips - 1, from_chip)
        high = col[...].astype(BF16)
        low = (col[...] - high.astype(F32)).astype(BF16)
        back = dot(high, weight[...], ((1,), (1,))) + dot(low, weight[...], ((1,), (1,)))
        loads[5 + rows_per].wait()
        col_ref[...] = (mask[...].astype(F32) * back).astype(BF16)

    def second(step):
        q = other_chip(step)
        two_copy(q, chip).start()

    if reduce_in:
        share = width // plane
        wg_part[...] = term[...].astype(BF16)

        def rs_copy(step):
            there, device = plane_id(step)
            return pltpu.make_async_remote_copy(
                src_ref=wg_part.at[pl.ds(pl.multiple_of(there * share, share), share)],
                dst_ref=rs_recv.at[step - 1],
                send_sem=rs_ssem.at[step - 1], recv_sem=rs_rsem.at[step - 1],
                device_id=device, device_id_type=MESH)

        for step in range(1, plane):
            rs_copy(step).start()
        each(chips - 1, second)
        forward()
        my_share = pl.ds(pl.multiple_of(place * share, share), share)
        total = term[my_share]
        for step in range(1, plane):
            rs_copy(step).wait_recv()
            total = total + rs_recv[step - 1].astype(F32)
        z_buf[my_z] = total.astype(BF16)

        def z_copy(step, slot):
            return pltpu.make_async_remote_copy(
                src_ref=z_buf.at[my_z], dst_ref=z_buf.at[slot],
                send_sem=z_ssem.at[step - 1], recv_sem=z_rsem.at[slot],
                device_id=z_id(step)[1], device_id_type=MESH)

        for step in range(1, z_size):
            z_copy(step, my_z).start()
        activate()
        for step in range(1, z_size):
            z_copy(step, z_id(step)[0]).wait_recv()
        total = z_buf[0].astype(F32)
        for z in range(1, z_size):
            total = total + z_buf[z].astype(F32)
        scale = 1.0 / math.sqrt(nodes * blk_size * rep_size)
        wg_full[my_share] = (total * scale).astype(BF16)

        def ag_copy(step, owner):
            rows = pl.ds(pl.multiple_of(owner * share, share), share)
            return pltpu.make_async_remote_copy(
                src_ref=wg_full.at[rows], dst_ref=wg_full.at[rows],
                send_sem=ag_ssem.at[step - 1], recv_sem=ag_rsem.at[step - 1],
                device_id=plane_id(step)[1], device_id_type=MESH)

        for step in range(1, plane):
            ag_copy(step, place).start()
        columns()
        for step in range(1, plane):
            ag_copy(step, lax.rem(place + plane - step, plane)).wait_recv()
        wg_ref[...] = wg_full[...].astype(F32)
    else:
        wg_ref[...] = term[...]
        each(chips - 1, second)
        forward()
        activate()
        columns()

    for piece in range(rows_per):
        each(chips - 1, lambda step: send_x(step, piece).wait_send())
        each(chips, lambda step: pass_on(other_chip(step), piece).wait_send())
    each(chips, lambda step: one_copy(other_chip(step)).wait_send())
    each(chips - 1, lambda step: two_copy(other_chip(step), chip).wait_send())
    if reduce_in:
        for step in range(1, plane):
            rs_copy(step).wait_send()
            ag_copy(step, place).wait_send()
        for step in range(1, z_size):
            z_copy(step, my_z).wait_send()


def write_out(a_ref, b_ref, c_ref, a_out, b_out, c_out, sem):
    copies = [pltpu.make_async_copy(src, dst, sem.at[i])
              for i, (src, dst) in enumerate(((a_ref, a_out), (b_ref, b_out), (c_ref, c_out)))]
    for copy in copies:
        copy.start()
    for copy in copies:
        copy.wait()


def per_device(features, weight, tile_values, tile_count, tile_cols, out_grad, relu_mask):
    rows_per, slots, tile = tile_values.shape[:3]
    width = features.shape[2]
    nodes = rows_per * tile
    blk_size, rep_size = lax.axis_size("blk"), lax.axis_size("rep")
    chips = blk_size // 2
    plane_y = 2
    z_size = rep_size // plane_y
    plane = blk_size * plane_y
    reduce_in = width % (plane * 16) == 0 and z_size <= 8
    share = width // plane if reduce_in else 16
    block = (nodes, width)
    dma = pltpu.SemaphoreType.DMA
    vmem = pltpu.VMEM
    scratch = [
        pltpu.SMEM((rows_per,), jnp.int32),
        pltpu.SMEM((rows_per, slots), jnp.int32),
        vmem(block, jnp.int32),
        vmem((rows_per, slots + 1, tile, tile), BF16),
        vmem(block, BF16),
        vmem((width, width), BF16),
        vmem((chips, 2 * nodes, width), BF16),
        vmem((chips, 2 * nodes, nodes), BF16),
        vmem((chips,) + block, F32),
        vmem((chips,) + block, BF16),
        vmem((chips,) + block, BF16),
        vmem((chips,) + block, BF16),
        vmem((chips,) + block, BF16),
        vmem(block, F32),
        vmem(block, F32),
        vmem((width, width), F32),
        vmem((width, width), BF16),
        vmem((plane - 1, share, width), BF16),
        vmem((z_size, share, width), BF16),
        vmem((width, width), BF16),
        dma((6 + rows_per,)),
        dma((chips, rows_per)), dma((2, chips, rows_per)), dma((chips, rows_per)),
        dma((chips,)), dma((chips,)), dma((chips,)), dma((chips,)),
        dma((plane - 1,)), dma((plane - 1,)), dma((z_size,)), dma((z_size,)),
        dma((plane - 1,)), dma((plane - 1,)),
    ]
    hbm = pl.BlockSpec(memory_space=pltpu.HBM)
    whole = pl.BlockSpec(memory_space=pltpu.VMEM)
    dims = (blk_size, rep_size, rows_per, slots, tile, width, plane_y, reduce_in)
    results = pl.pallas_call(
        functools.partial(kernel, dims),
        out_shape=(
            jax.ShapeDtypeStruct(block, BF16),
            jax.ShapeDtypeStruct(block, BF16),
            jax.ShapeDtypeStruct((width, width), F32),
        ),
        in_specs=[hbm] * 7,
        out_specs=(whole, whole, whole),
        scratch_shapes=scratch,
        compiler_params=pltpu.CompilerParams(
            collective_id=0, has_side_effects=True, vmem_limit_bytes=32 * 1024 * 1024
        ),
        name="layer",
    )(*[pltpu.with_memory_space_constraint(x, pltpu.HBM) for x in (
        tile_count, tile_cols, features.reshape(block), tile_values, out_grad.reshape(block), weight,
        relu_mask.reshape(block))])
    activated, in_grad, weight_term = pl.pallas_call(
        write_out,
        out_shape=tuple(jax.ShapeDtypeStruct(r.shape, r.dtype) for r in results),
        in_specs=[whole] * 3,
        out_specs=(hbm, hbm, hbm),
        scratch_shapes=[dma((3,))],
        compiler_params=pltpu.CompilerParams(vmem_limit_bytes=4 * 1024 * 1024),
        name="write_out",
    )(*results)
    activated, in_grad = activated.reshape(features.shape), in_grad.reshape(features.shape)
    if not reduce_in:
        scale = 1.0 / math.sqrt(nodes * blk_size * rep_size)
        weight_term = lax.psum(weight_term, ("blk", "rep")) * scale
    return (activated, weight_term, in_grad)


def solution(mesh):
    placed = (
        P(("blk", "rep"), None, None),
        P(),
        P(("blk", "rep"), None, None, None),
        P(("blk", "rep")),
        P(("blk", "rep"), None),
        P(("blk", "rep"), None, None),
        P(("blk", "rep"), None, None),
    )
    return jax.shard_map(
        per_device,
        mesh=mesh,
        in_specs=placed,
        out_specs=(P(("blk", "rep"), None, None), P(), P(("blk", "rep"), None, None)),
        check_vma=False,
    )
```

```python
import functools
import math

import jax
import jax.numpy as jnp
from jax import lax
from jax.experimental import pallas as pl
from jax.experimental.pallas import tpu as pltpu
from jax.sharding import PartitionSpec as P

MESH = pl.DeviceIdType.MESH
BF16 = jnp.bfloat16
F32 = jnp.float32


def each(count, body):
    if count <= 2:
        for step in range(count):
            body(step)
    else:
        lax.fori_loop(0, count, lambda step, carry: (body(step), carry)[1], 0)


def dot(a, b, contract=((1,), (0,))):
    return lax.dot_general(a, b, (contract, ((), ())), preferred_element_type=F32)


def kernel(dims, *refs):
    blk_size, rep_size, rows_per, slots, tile, width, plane_y, reduce_in = dims
    (count_hbm, cols_hbm, feat_ref, tv_ref, grad_ref, weight_ref, mask_ref) = refs[:7]
    (act_ref, col_ref, wg_ref) = refs[7:10]
    (count_ref, cols_ref, mask, tv, grad, weight, feats, dense, own, one_send, one_recv, two_send, two_recv,
     act, col, term, wg_part, rs_recv, z_buf, wg_full,
     in_sem, f_send, f_recv, fwd_send, one_ssem, one_rsem, two_ssem, two_rsem,
     rs_ssem, rs_rsem, z_ssem, z_rsem, ag_ssem, ag_rsem) = refs[10:]
    nodes, half = rows_per * tile, width // 2
    chips = blk_size // 2
    z_size = rep_size // plane_y
    plane = blk_size * plane_y
    blk, rep = lax.axis_index("blk"), lax.axis_index("rep")
    chip, core = blk // 2, lax.rem(blk, 2)
    sib = chip * 2 + 1 - core
    my_y, my_z = lax.rem(rep, plane_y), rep // plane_y
    place = my_y * blk_size + blk

    def other_chip(step):
        return lax.rem(chip + 1 + step, chips)

    def plane_id(step):
        there = lax.rem(place + step, plane)
        return there, {"blk": lax.rem(there, blk_size), "rep": my_z * plane_y + there // blk_size}

    def z_id(step):
        there = lax.rem(my_z + step, z_size)
        return there, {"blk": blk, "rep": there * plane_y + my_y}

    barrier = pltpu.get_barrier_semaphore()
    if reduce_in:
        for step in range(1, plane):
            pl.semaphore_signal(barrier, inc=1, device_id=plane_id(step)[1], device_id_type=MESH)
        for step in range(1, z_size):
            pl.semaphore_signal(barrier, inc=1, device_id=z_id(step)[1], device_id_type=MESH)
        greeted = plane - 1 + z_size - 1
    else:
        pl.semaphore_signal(barrier, inc=1, device_id={"blk": sib, "rep": rep}, device_id_type=MESH)
        for step in range(chips - 1):
            pl.semaphore_signal(
                barrier, inc=1, device_id={"blk": other_chip(step) * 2 + core, "rep": rep}, device_id_type=MESH)
        greeted = chips

    loads = [pltpu.make_async_copy(grad_ref, grad, in_sem.at[0]),
             pltpu.make_async_copy(weight_ref, weight, in_sem.at[1])]
    for t in range(rows_per):
        loads.append(pltpu.make_async_copy(tv_ref.at[t], tv.at[t, pl.ds(0, slots)], in_sem.at[2 + t]))
    my_rows = pl.ds(pl.multiple_of(core * nodes, nodes), nodes)
    sib_rows = pl.ds(pl.multiple_of((1 - core) * nodes, nodes), nodes)
    loads.append(pltpu.make_async_copy(feat_ref, feats.at[chip, my_rows], in_sem.at[2 + rows_per]))
    loads.append(pltpu.make_async_copy(count_hbm, count_ref, in_sem.at[3 + rows_per]))
    loads.append(pltpu.make_async_copy(cols_hbm, cols_ref, in_sem.at[4 + rows_per]))
    loads.append(pltpu.make_async_copy(mask_ref, mask, in_sem.at[5 + rows_per]))
    for i in [3 + rows_per, 4 + rows_per] + list(range(2, 2 + rows_per)) + [0, 2 + rows_per]:
        loads[i].start()
    pl.semaphore_wait(barrier, greeted)

    def x_copy(origin, device, piece):
        lanes = pl.ds(piece * half, half)
        return pltpu.make_async_remote_copy(
            src_ref=feat_ref.at[:, lanes], dst_ref=feats.at[origin, my_rows, lanes],
            send_sem=f_send.at[device // 2, piece], recv_sem=f_recv.at[0, origin, piece],
            device_id={"blk": device, "rep": rep}, device_id_type=MESH)

    def send_x(step, piece):
        return x_copy(chip, other_chip(step) * 2 + core, piece)

    def came_x(q, piece):
        return x_copy(q, q * 2 + core, piece)

    def sib_copy(q, rows, piece):
        lanes = pl.ds(piece * half, half)
        return pltpu.make_async_remote_copy(
            src_ref=feats.at[q, rows, lanes], dst_ref=feats.at[q, rows, lanes],
            send_sem=fwd_send.at[q, piece], recv_sem=f_recv.at[1, q, piece],
            device_id={"blk": sib, "rep": rep}, device_id_type=MESH)

    def pass_on(q, piece):
        return sib_copy(q, my_rows, piece)

    def passed(q, piece):
        return sib_copy(q, sib_rows, piece)

    for piece in range(2):
        each(chips - 1, lambda step: send_x(step, piece).start())
    loads[1].start()
    loads[5 + rows_per].start()
    loads[2 + rows_per].wait()
    for piece in range(2):
        pass_on(chip, piece).start()

    loads[3 + rows_per].wait()
    loads[4 + rows_per].wait()
    loads[0].wait()
    for t in range(rows_per):
        loads[2 + t].wait()
        tv[t, slots] = jnp.zeros((tile, tile), BF16)

    used = [[jnp.where(s < count_ref[t], cols_ref[t, s], -1) for s in range(slots)] for t in range(rows_per)]

    def block_of(q, c):
        member = q * 2 + c
        bands = []
        for r in range(rows_per):
            column = (member * rep_size + rep) * rows_per + r
            pieces = []
            for t in range(rows_per):
                slot = jnp.int32(slots)
                for s in range(slots):
                    slot = jnp.where(used[t][s] == column, jnp.int32(s), slot)
                pieces.append(tv[t, slot])
            bands.append(jnp.concatenate(pieces, axis=1))
        return jnp.concatenate(bands, axis=0)

    def one_copy(q):
        return pltpu.make_async_remote_copy(
            src_ref=one_send.at[q], dst_ref=one_recv.at[q],
            send_sem=one_ssem.at[q], recv_sem=one_rsem.at[q],
            device_id={"blk": sib, "rep": rep}, device_id_type=MESH)

    def two_copy(q, slot):
        return pltpu.make_async_remote_copy(
            src_ref=two_send.at[q], dst_ref=two_recv.at[slot],
            send_sem=two_ssem.at[q], recv_sem=two_rsem.at[slot],
            device_id={"blk": q * 2 + core, "rep": rep}, device_id_type=MESH)

    def for_sibling(step):
        q = other_chip(step)
        block = block_of(q, 1 - core)
        one_send[q] = dot(block, grad[...]).astype(BF16)
        one_copy(q).start()
        dense[q, sib_rows] = block

    def for_core(step):
        q = other_chip(step)
        block = block_of(q, core)
        own[q] = dot(block, grad[...])
        dense[q, my_rows] = block

    def pair(step):
        q = other_chip(step)
        one_copy(q).wait_recv()
        total = own[q] + one_recv[q].astype(F32)
        own[q] = total
        two_send[q] = total.astype(BF16)

    each(chips, for_sibling)
    each(chips, for_core)
    each(chips, pair)

    term[...] = dot(feats[chip, my_rows], two_send[chip], ((0,), (0,)))

    def arrive(piece):
        rows = pl.ds(piece * half, half)

        def from_chip(step):
            q = other_chip(step)
            came_x(q, piece).wait_recv()
            pass_on(q, piece).start()
            term[rows] += dot(feats[q, my_rows, rows], two_send[q], ((0,), (0,)))

        each(chips - 1, from_chip)

    def forward():
        for piece in range(2):
            passed(chip, piece).wait_recv()
        act[...] = dot(dense[chip], feats[chip], ((0,), (0,)))

        def from_chip(step):
            q = other_chip(step)
            for piece in range(2):
                passed(q, piece).wait_recv()
            act[...] += dot(dense[q], feats[q], ((0,), (0,)))

        each(chips - 1, from_chip)

    def activate():
        loads[1].wait()
        act_ref[...] = jnp.maximum(dot(act[...].astype(BF16), weight[...]), 0.0).astype(BF16)

    def columns():
        col[...] = own[chip]

        def from_chip(step):
            q = other_chip(step)
            two_copy(q, q).wait_recv()
            col[...] += two_recv[q].astype(F32)

        each(chips - 1, from_chip)
        high = col[...].astype(BF16)
        low = (col[...] - high.astype(F32)).astype(BF16)
        back = dot(high, weight[...], ((1,), (1,))) + dot(low, weight[...], ((1,), (1,)))
        loads[5 + rows_per].wait()
        col_ref[...] = (mask[...].astype(F32) * back).astype(BF16)

    def second(step):
        q = other_chip(step)
        two_copy(q, chip).start()

    if reduce_in:
        share = half // plane
        scale = 1.0 / math.sqrt(nodes * blk_size * rep_size)

        def rows_of(piece, owner):
            return pl.ds(pl.multiple_of(piece * half + owner * share, share), share)

        def rs_copy(piece, step):
            there, device = plane_id(step)
            return pltpu.make_async_remote_copy(
                src_ref=wg_part.at[rows_of(piece, there)], dst_ref=rs_recv.at[piece, step - 1],
                send_sem=rs_ssem.at[piece, step - 1], recv_sem=rs_rsem.at[piece, step - 1],
                device_id=device, device_id_type=MESH)

        def z_copy(piece, step, slot):
            return pltpu.make_async_remote_copy(
                src_ref=z_buf.at[piece, my_z], dst_ref=z_buf.at[piece, slot],
                send_sem=z_ssem.at[piece, step - 1], recv_sem=z_rsem.at[piece, slot],
                device_id=z_id(step)[1], device_id_type=MESH)

        def ag_copy(piece, step, owner):
            rows = rows_of(piece, owner)
            return pltpu.make_async_remote_copy(
                src_ref=wg_full.at[rows], dst_ref=wg_full.at[rows],
                send_sem=ag_ssem.at[piece, step - 1], recv_sem=ag_rsem.at[piece, step - 1],
                device_id=plane_id(step)[1], device_id_type=MESH)

        for piece in range(2):
            arrive(piece)
            rows = pl.ds(piece * half, half)
            wg_part[rows] = term[rows].astype(BF16)
            for step in range(1, plane):
                rs_copy(piece, step).start()
        each(chips - 1, second)
        for piece in range(2):
            total = term[rows_of(piece, place)]
            for step in range(1, plane):
                rs_copy(piece, step).wait_recv()
                total = total + rs_recv[piece, step - 1].astype(F32)
            z_buf[piece, my_z] = total.astype(BF16)
            for step in range(1, z_size):
                z_copy(piece, step, my_z).start()
        forward()
        for piece in range(2):
            for step in range(1, z_size):
                z_copy(piece, step, z_id(step)[0]).wait_recv()
            total = z_buf[piece, 0].astype(F32)
            for z in range(1, z_size):
                total = total + z_buf[piece, z].astype(F32)
            wg_full[rows_of(piece, place)] = (total * scale).astype(BF16)
            for step in range(1, plane):
                ag_copy(piece, step, place).start()
            if piece == 0:
                activate()
        columns()
        for piece in range(2):
            for step in range(1, plane):
                ag_copy(piece, step, lax.rem(place + plane - step, plane)).wait_recv()
            rows = pl.ds(piece * half, half)
            wg_ref[rows] = wg_full[rows].astype(F32)
    else:
        for piece in range(2):
            arrive(piece)
        wg_ref[...] = term[...]
        each(chips - 1, second)
        forward()
        activate()
        columns()

    for piece in range(2):
        each(chips - 1, lambda step: send_x(step, piece).wait_send())
        each(chips, lambda step: pass_on(other_chip(step), piece).wait_send())
    each(chips, lambda step: one_copy(other_chip(step)).wait_send())
    each(chips - 1, lambda step: two_copy(other_chip(step), chip).wait_send())
    if reduce_in:
        for piece in range(2):
            for step in range(1, plane):
                rs_copy(piece, step).wait_send()
                ag_copy(piece, step, place).wait_send()
            for step in range(1, z_size):
                z_copy(piece, step, my_z).wait_send()


def write_out(a_ref, b_ref, c_ref, a_out, b_out, c_out, sem):
    copies = [pltpu.make_async_copy(src, dst, sem.at[i])
              for i, (src, dst) in enumerate(((a_ref, a_out), (b_ref, b_out), (c_ref, c_out)))]
    for copy in copies:
        copy.start()
    for copy in copies:
        copy.wait()


def per_device(features, weight, tile_values, tile_count, tile_cols, out_grad, relu_mask):
    rows_per, slots, tile = tile_values.shape[:3]
    width = features.shape[2]
    nodes = rows_per * tile
    blk_size, rep_size = lax.axis_size("blk"), lax.axis_size("rep")
    chips = blk_size // 2
    plane_y = 2
    z_size = rep_size // plane_y
    plane = blk_size * plane_y
    reduce_in = width % (plane * 32) == 0 and z_size <= 8
    share = width // 2 // plane if reduce_in else 16
    block = (nodes, width)
    dma = pltpu.SemaphoreType.DMA
    vmem = pltpu.VMEM
    scratch = [
        pltpu.SMEM((rows_per,), jnp.int32),
        pltpu.SMEM((rows_per, slots), jnp.int32),
        vmem(block, jnp.int32),
        vmem((rows_per, slots + 1, tile, tile), BF16),
        vmem(block, BF16),
        vmem((width, width), BF16),
        vmem((chips, 2 * nodes, width), BF16),
        vmem((chips, 2 * nodes, nodes), BF16),
        vmem((chips,) + block, F32),
        vmem((chips,) + block, BF16),
        vmem((chips,) + block, BF16),
        vmem((chips,) + block, BF16),
        vmem((chips,) + block, BF16),
        vmem(block, F32),
        vmem(block, F32),
        vmem((width, width), F32),
        vmem((width, width), BF16),
        vmem((2, plane - 1, share, width), BF16),
        vmem((2, z_size, share, width), BF16),
        vmem((width, width), BF16),
        dma((6 + rows_per,)),
        dma((chips, 2)), dma((2, chips, 2)), dma((chips, 2)),
        dma((chips,)), dma((chips,)), dma((chips,)), dma((chips,)),
        dma((2, plane - 1)), dma((2, plane - 1)), dma((2, z_size)), dma((2, z_size)),
        dma((2, plane - 1)), dma((2, plane - 1)),
    ]
    hbm = pl.BlockSpec(memory_space=pltpu.HBM)
    whole = pl.BlockSpec(memory_space=pltpu.VMEM)
    dims = (blk_size, rep_size, rows_per, slots, tile, width, plane_y, reduce_in)
    results = pl.pallas_call(
        functools.partial(kernel, dims),
        out_shape=(
            jax.ShapeDtypeStruct(block, BF16),
            jax.ShapeDtypeStruct(block, BF16),
            jax.ShapeDtypeStruct((width, width), F32),
        ),
        in_specs=[hbm] * 7,
        out_specs=(whole, whole, whole),
        scratch_shapes=scratch,
        compiler_params=pltpu.CompilerParams(
            collective_id=0, has_side_effects=True, vmem_limit_bytes=32 * 1024 * 1024
        ),
        name="layer",
    )(*[pltpu.with_memory_space_constraint(x, pltpu.HBM) for x in (
        tile_count, tile_cols, features.reshape(block), tile_values, out_grad.reshape(block), weight,
        relu_mask.reshape(block))])
    activated, in_grad, weight_term = pl.pallas_call(
        write_out,
        out_shape=tuple(jax.ShapeDtypeStruct(r.shape, r.dtype) for r in results),
        in_specs=[whole] * 3,
        out_specs=(hbm, hbm, hbm),
        scratch_shapes=[dma((3,))],
        compiler_params=pltpu.CompilerParams(vmem_limit_bytes=4 * 1024 * 1024),
        name="write_out",
    )(*results)
    activated, in_grad = activated.reshape(features.shape), in_grad.reshape(features.shape)
    if not reduce_in:
        scale = 1.0 / math.sqrt(nodes * blk_size * rep_size)
        weight_term = lax.psum(weight_term, ("blk", "rep")) * scale
    return (activated, weight_term, in_grad)


def solution(mesh):
    placed = (
        P(("blk", "rep"), None, None),
        P(),
        P(("blk", "rep"), None, None, None),
        P(("blk", "rep")),
        P(("blk", "rep"), None),
        P(("blk", "rep"), None, None),
        P(("blk", "rep"), None, None),
    )
    return jax.shard_map(
        per_device,
        mesh=mesh,
        in_specs=placed,
        out_specs=(P(("blk", "rep"), None, None), P(), P(("blk", "rep"), None, None)),
        check_vma=False,
    )
```

```python
import functools
import math

import jax
import jax.numpy as jnp
from jax import lax
from jax.experimental import pallas as pl
from jax.experimental.pallas import tpu as pltpu
from jax.sharding import PartitionSpec as P

MESH = pl.DeviceIdType.MESH
BF16 = jnp.bfloat16
F32 = jnp.float32


def each(count, body):
    if count <= 2:
        for step in range(count):
            body(step)
    else:
        lax.fori_loop(0, count, lambda step, carry: (body(step), carry)[1], 0)


def dot(a, b, contract=((1,), (0,))):
    return lax.dot_general(a, b, (contract, ((), ())), preferred_element_type=F32)


def kernel(dims, *refs):
    blk_size, rep_size, rows_per, slots, tile, width, plane_y, reduce_in = dims
    (count_hbm, cols_hbm, feat_ref, tv_ref, grad_ref, weight_ref, mask_ref) = refs[:7]
    (act_ref, col_ref, wg_ref) = refs[7:10]
    (count_ref, cols_ref, mask, tv, grad, weight, feats, dense, own, one_send, one_recv, two_send, two_recv,
     act, col, term, wg_part, rs_recv, z_buf, wg_full,
     in_sem, f_send, f_recv, fwd_send, one_ssem, one_rsem, two_ssem, two_rsem,
     rs_ssem, rs_rsem, z_ssem, z_rsem, ag_ssem, ag_rsem) = refs[10:]
    nodes, half = rows_per * tile, width // 2
    chips = blk_size // 2
    z_size = rep_size // plane_y
    plane = blk_size * plane_y
    blk, rep = lax.axis_index("blk"), lax.axis_index("rep")
    chip, core = blk // 2, lax.rem(blk, 2)
    sib = chip * 2 + 1 - core
    my_y, my_z = lax.rem(rep, plane_y), rep // plane_y
    place = my_y * blk_size + blk

    def other_chip(step):
        return lax.rem(chip + 1 + step, chips)

    def plane_id(step):
        there = lax.rem(place + step, plane)
        return there, {"blk": lax.rem(there, blk_size), "rep": my_z * plane_y + there // blk_size}

    def z_id(step):
        there = lax.rem(my_z + step, z_size)
        return there, {"blk": blk, "rep": there * plane_y + my_y}

    barrier = pltpu.get_barrier_semaphore()
    if reduce_in:
        for step in sorted(range(1, plane), key=lambda s: min(s, plane - s)):
            pl.semaphore_signal(barrier, inc=1, device_id=plane_id(step)[1], device_id_type=MESH)
        for step in range(1, z_size):
            pl.semaphore_signal(barrier, inc=1, device_id=z_id(step)[1], device_id_type=MESH)
        greeted = plane - 1 + z_size - 1
    else:
        pl.semaphore_signal(barrier, inc=1, device_id={"blk": sib, "rep": rep}, device_id_type=MESH)
        for step in range(chips - 1):
            pl.semaphore_signal(
                barrier, inc=1, device_id={"blk": other_chip(step) * 2 + core, "rep": rep}, device_id_type=MESH)
        greeted = chips

    loads = [pltpu.make_async_copy(grad_ref, grad, in_sem.at[0]),
             pltpu.make_async_copy(weight_ref, weight, in_sem.at[1])]
    for t in range(rows_per):
        loads.append(pltpu.make_async_copy(tv_ref.at[t], tv.at[t, pl.ds(0, slots)], in_sem.at[2 + t]))
    my_rows = pl.ds(pl.multiple_of(core * nodes, nodes), nodes)
    sib_rows = pl.ds(pl.multiple_of((1 - core) * nodes, nodes), nodes)
    loads.append(pltpu.make_async_copy(feat_ref, feats.at[chip, my_rows], in_sem.at[2 + rows_per]))
    loads.append(pltpu.make_async_copy(count_hbm, count_ref, in_sem.at[3 + rows_per]))
    loads.append(pltpu.make_async_copy(cols_hbm, cols_ref, in_sem.at[4 + rows_per]))
    loads.append(pltpu.make_async_copy(mask_ref, mask, in_sem.at[5 + rows_per]))
    for i in [3 + rows_per, 4 + rows_per] + list(range(2, 2 + rows_per)) + [0, 2 + rows_per]:
        loads[i].start()
    pl.semaphore_wait(barrier, greeted)

    def x_copy(origin, device, piece):
        lanes = pl.ds(piece * half, half)
        return pltpu.make_async_remote_copy(
            src_ref=feat_ref.at[:, lanes], dst_ref=feats.at[origin, my_rows, lanes],
            send_sem=f_send.at[device // 2, piece], recv_sem=f_recv.at[0, origin, piece],
            device_id={"blk": device, "rep": rep}, device_id_type=MESH)

    def send_x(step, piece):
        return x_copy(chip, other_chip(step) * 2 + core, piece)

    def came_x(q, piece):
        return x_copy(q, q * 2 + core, piece)

    def sib_copy(q, rows, piece):
        lanes = pl.ds(piece * half, half)
        return pltpu.make_async_remote_copy(
            src_ref=feats.at[q, rows, lanes], dst_ref=feats.at[q, rows, lanes],
            send_sem=fwd_send.at[q, piece], recv_sem=f_recv.at[1, q, piece],
            device_id={"blk": sib, "rep": rep}, device_id_type=MESH)

    def pass_on(q, piece):
        return sib_copy(q, my_rows, piece)

    def passed(q, piece):
        return sib_copy(q, sib_rows, piece)

    for piece in range(2):
        each(chips - 1, lambda step: send_x(step, piece).start())
    loads[1].start()
    loads[5 + rows_per].start()
    loads[2 + rows_per].wait()
    for piece in range(2):
        pass_on(chip, piece).start()

    loads[3 + rows_per].wait()
    loads[4 + rows_per].wait()
    loads[0].wait()
    for t in range(rows_per):
        loads[2 + t].wait()
        tv[t, slots] = jnp.zeros((tile, tile), BF16)

    used = [[jnp.where(s < count_ref[t], cols_ref[t, s], -1) for s in range(slots)] for t in range(rows_per)]

    def block_of(q, c):
        member = q * 2 + c
        bands = []
        for r in range(rows_per):
            column = (member * rep_size + rep) * rows_per + r
            pieces = []
            for t in range(rows_per):
                slot = jnp.int32(slots)
                for s in range(slots):
                    slot = jnp.where(used[t][s] == column, jnp.int32(s), slot)
                pieces.append(tv[t, slot])
            bands.append(jnp.concatenate(pieces, axis=1))
        return jnp.concatenate(bands, axis=0)

    def one_copy(q):
        return pltpu.make_async_remote_copy(
            src_ref=one_send.at[q], dst_ref=one_recv.at[q],
            send_sem=one_ssem.at[q], recv_sem=one_rsem.at[q],
            device_id={"blk": sib, "rep": rep}, device_id_type=MESH)

    def two_copy(q, slot):
        return pltpu.make_async_remote_copy(
            src_ref=two_send.at[q], dst_ref=two_recv.at[slot],
            send_sem=two_ssem.at[q], recv_sem=two_rsem.at[slot],
            device_id={"blk": q * 2 + core, "rep": rep}, device_id_type=MESH)

    def for_sibling(step):
        q = other_chip(step)
        block = block_of(q, 1 - core)
        one_send[q] = dot(block, grad[...]).astype(BF16)
        one_copy(q).start()
        dense[q, sib_rows] = block

    def for_core(step):
        q = other_chip(step)
        block = block_of(q, core)
        own[q] = dot(block, grad[...])
        dense[q, my_rows] = block

    def pair(step):
        q = other_chip(step)
        one_copy(q).wait_recv()
        total = own[q] + one_recv[q].astype(F32)
        own[q] = total
        two_send[q] = total.astype(BF16)

    each(chips, for_sibling)
    each(chips, for_core)
    each(chips, pair)

    def arrive(piece):
        rows = pl.ds(piece * half, half)
        term[rows] = dot(feats[chip, my_rows, rows], two_send[chip], ((0,), (0,)))

        def from_chip(step):
            q = other_chip(step)
            came_x(q, piece).wait_recv()
            pass_on(q, piece).start()
            term[rows] += dot(feats[q, my_rows, rows], two_send[q], ((0,), (0,)))

        each(chips - 1, from_chip)

    def forward():
        for piece in range(2):
            passed(chip, piece).wait_recv()
        act[...] = dot(dense[chip], feats[chip], ((0,), (0,)))

        def from_chip(step):
            q = other_chip(step)
            for piece in range(2):
                passed(q, piece).wait_recv()
            act[...] += dot(dense[q], feats[q], ((0,), (0,)))

        each(chips - 1, from_chip)

    def activate():
        loads[1].wait()
        act_ref[...] = jnp.maximum(dot(act[...].astype(BF16), weight[...]), 0.0).astype(BF16)

    def columns():
        col[...] = own[chip]

        def from_chip(step):
            q = other_chip(step)
            two_copy(q, q).wait_recv()
            col[...] += two_recv[q].astype(F32)

        each(chips - 1, from_chip)
        high = col[...].astype(BF16)
        low = (col[...] - high.astype(F32)).astype(BF16)
        back = dot(high, weight[...], ((1,), (1,))) + dot(low, weight[...], ((1,), (1,)))
        loads[5 + rows_per].wait()
        col_ref[...] = (mask[...].astype(F32) * back).astype(BF16)

    def second(step):
        q = other_chip(step)
        two_copy(q, chip).start()

    def sent():
        for piece in range(2):
            each(chips - 1, lambda step: send_x(step, piece).wait_send())
            each(chips, lambda step: pass_on(other_chip(step), piece).wait_send())
        each(chips, lambda step: one_copy(other_chip(step)).wait_send())
        each(chips - 1, lambda step: two_copy(other_chip(step), chip).wait_send())

    if reduce_in:
        share = half // plane
        scale = 1.0 / math.sqrt(nodes * blk_size * rep_size)

        def rows_of(piece, owner):
            return pl.ds(pl.multiple_of(piece * half + owner * share, share), share)

        def rs_copy(piece, step):
            there, device = plane_id(step)
            return pltpu.make_async_remote_copy(
                src_ref=wg_part.at[rows_of(piece, there)], dst_ref=rs_recv.at[piece, step - 1],
                send_sem=rs_ssem.at[piece, step - 1], recv_sem=rs_rsem.at[piece, step - 1],
                device_id=device, device_id_type=MESH)

        def z_copy(piece, step, slot):
            return pltpu.make_async_remote_copy(
                src_ref=z_buf.at[piece, my_z], dst_ref=z_buf.at[piece, slot],
                send_sem=z_ssem.at[piece, step - 1], recv_sem=z_rsem.at[piece, slot],
                device_id=z_id(step)[1], device_id_type=MESH)

        def ag_copy(piece, step, owner):
            rows = rows_of(piece, owner)
            return pltpu.make_async_remote_copy(
                src_ref=wg_full.at[rows], dst_ref=wg_full.at[rows],
                send_sem=ag_ssem.at[piece, step - 1], recv_sem=ag_rsem.at[piece, step - 1],
                device_id=plane_id(step)[1], device_id_type=MESH)

        for piece in range(2):
            arrive(piece)
            rows = pl.ds(piece * half, half)
            wg_part[rows] = term[rows].astype(BF16)
            for step in range(1, plane):
                rs_copy(piece, step).start()
        for piece in range(2):
            total = term[rows_of(piece, place)]
            for step in range(1, plane):
                rs_copy(piece, step).wait_recv()
                total = total + rs_recv[piece, step - 1].astype(F32)
            z_buf[piece, my_z] = total.astype(BF16)
            for step in range(1, z_size):
                z_copy(piece, step, my_z).start()
        each(chips - 1, second)
        forward()
        for piece in range(2):
            for step in range(1, z_size):
                z_copy(piece, step, z_id(step)[0]).wait_recv()
            total = z_buf[piece, 0].astype(F32)
            for z in range(1, z_size):
                total = total + z_buf[piece, z].astype(F32)
            wg_full[rows_of(piece, place)] = (total * scale).astype(BF16)
            for step in range(1, plane):
                ag_copy(piece, step, place).start()
            if piece == 0:
                activate()
        columns()
        sent()
        for piece in range(2):
            for step in range(1, plane):
                rs_copy(piece, step).wait_send()
                ag_copy(piece, step, place).wait_send()
            for step in range(1, z_size):
                z_copy(piece, step, my_z).wait_send()
        for piece in range(2):
            for step in range(1, plane):
                ag_copy(piece, step, lax.rem(place + plane - step, plane)).wait_recv()
            rows = pl.ds(piece * half, half)
            wg_ref[rows] = wg_full[rows].astype(F32)
    else:
        for piece in range(2):
            arrive(piece)
        wg_ref[...] = term[...]
        each(chips - 1, second)
        forward()
        activate()
        columns()
        sent()


def write_out(a_ref, b_ref, c_ref, a_out, b_out, c_out, sem):
    copies = [pltpu.make_async_copy(src, dst, sem.at[i])
              for i, (src, dst) in enumerate(((a_ref, a_out), (b_ref, b_out), (c_ref, c_out)))]
    for copy in copies:
        copy.start()
    for copy in copies:
        copy.wait()


def per_device(features, weight, tile_values, tile_count, tile_cols, out_grad, relu_mask):
    rows_per, slots, tile = tile_values.shape[:3]
    width = features.shape[2]
    nodes = rows_per * tile
    blk_size, rep_size = lax.axis_size("blk"), lax.axis_size("rep")
    chips = blk_size // 2
    plane_y = 2
    z_size = rep_size // plane_y
    plane = blk_size * plane_y
    reduce_in = width % (plane * 32) == 0 and z_size <= 8
    share = width // 2 // plane if reduce_in else 16
    block = (nodes, width)
    dma = pltpu.SemaphoreType.DMA
    vmem = pltpu.VMEM
    scratch = [
        pltpu.SMEM((rows_per,), jnp.int32),
        pltpu.SMEM((rows_per, slots), jnp.int32),
        vmem(block, jnp.int32),
        vmem((rows_per, slots + 1, tile, tile), BF16),
        vmem(block, BF16),
        vmem((width, width), BF16),
        vmem((chips, 2 * nodes, width), BF16),
        vmem((chips, 2 * nodes, nodes), BF16),
        vmem((chips,) + block, F32),
        vmem((chips,) + block, BF16),
        vmem((chips,) + block, BF16),
        vmem((chips,) + block, BF16),
        vmem((chips,) + block, BF16),
        vmem(block, F32),
        vmem(block, F32),
        vmem((width, width), F32),
        vmem((width, width), BF16),
        vmem((2, plane - 1, share, width), BF16),
        vmem((2, z_size, share, width), BF16),
        vmem((width, width), BF16),
        dma((6 + rows_per,)),
        dma((chips, 2)), dma((2, chips, 2)), dma((chips, 2)),
        dma((chips,)), dma((chips,)), dma((chips,)), dma((chips,)),
        dma((2, plane - 1)), dma((2, plane - 1)), dma((2, z_size)), dma((2, z_size)),
        dma((2, plane - 1)), dma((2, plane - 1)),
    ]
    hbm = pl.BlockSpec(memory_space=pltpu.HBM)
    whole = pl.BlockSpec(memory_space=pltpu.VMEM)
    dims = (blk_size, rep_size, rows_per, slots, tile, width, plane_y, reduce_in)
    results = pl.pallas_call(
        functools.partial(kernel, dims),
        out_shape=(
            jax.ShapeDtypeStruct(block, BF16),
            jax.ShapeDtypeStruct(block, BF16),
            jax.ShapeDtypeStruct((width, width), F32),
        ),
        in_specs=[hbm] * 7,
        out_specs=(whole, whole, whole),
        scratch_shapes=scratch,
        compiler_params=pltpu.CompilerParams(
            collective_id=0, has_side_effects=True, vmem_limit_bytes=32 * 1024 * 1024
        ),
        name="layer",
    )(*[pltpu.with_memory_space_constraint(x, pltpu.HBM) for x in (
        tile_count, tile_cols, features.reshape(block), tile_values, out_grad.reshape(block), weight,
        relu_mask.reshape(block))])
    activated, in_grad, weight_term = pl.pallas_call(
        write_out,
        out_shape=tuple(jax.ShapeDtypeStruct(r.shape, r.dtype) for r in results),
        in_specs=[whole] * 3,
        out_specs=(hbm, hbm, hbm),
        scratch_shapes=[dma((3,))],
        compiler_params=pltpu.CompilerParams(vmem_limit_bytes=4 * 1024 * 1024),
        name="write_out",
    )(*results)
    activated, in_grad = activated.reshape(features.shape), in_grad.reshape(features.shape)
    if not reduce_in:
        scale = 1.0 / math.sqrt(nodes * blk_size * rep_size)
        weight_term = lax.psum(weight_term, ("blk", "rep")) * scale
    return (activated, weight_term, in_grad)


def solution(mesh):
    placed = (
        P(("blk", "rep"), None, None),
        P(),
        P(("blk", "rep"), None, None, None),
        P(("blk", "rep")),
        P(("blk", "rep"), None),
        P(("blk", "rep"), None, None),
        P(("blk", "rep"), None, None),
    )
    return jax.shard_map(
        per_device,
        mesh=mesh,
        in_specs=placed,
        out_specs=(P(("blk", "rep"), None, None), P(), P(("blk", "rep"), None, None)),
        check_vma=False,
    )
```

```python
import functools
import math

import jax
import jax.numpy as jnp
from jax import lax
from jax.experimental import pallas as pl
from jax.experimental.pallas import tpu as pltpu
from jax.sharding import PartitionSpec as P

MESH = pl.DeviceIdType.MESH
BF16 = jnp.bfloat16
F32 = jnp.float32


def each(count, body):
    if count <= 2:
        for step in range(count):
            body(step)
    else:
        lax.fori_loop(0, count, lambda step, carry: (body(step), carry)[1], 0)


def dot(a, b, contract=((1,), (0,))):
    return lax.dot_general(a, b, (contract, ((), ())), preferred_element_type=F32)


def kernel(dims, *refs):
    blk_size, rep_size, rows_per, slots, tile, width, plane_y, reduce_in = dims
    (count_hbm, cols_hbm, feat_ref, tv_ref, grad_ref, weight_ref, mask_ref) = refs[:7]
    (act_ref, col_ref, wg_ref) = refs[7:10]
    (count_ref, cols_ref, mask, tv, grad, weight, feats, dense, own, one_send, one_recv, two_send, two_recv,
     act, col, term, wg_part, rs_recv, z_buf, wg_full,
     in_sem, f_send, f_recv, fwd_send, one_ssem, one_rsem, two_ssem, two_rsem,
     rs_ssem, rs_rsem, z_ssem, z_rsem, ag_ssem, ag_rsem) = refs[10:]
    nodes, half = rows_per * tile, width // 2
    chips = blk_size // 2
    z_size = rep_size // plane_y
    plane = blk_size * plane_y
    blk, rep = lax.axis_index("blk"), lax.axis_index("rep")
    chip, core = blk // 2, lax.rem(blk, 2)
    sib = chip * 2 + 1 - core
    my_y, my_z = lax.rem(rep, plane_y), rep // plane_y
    place = my_y * blk_size + blk

    def other_chip(step):
        return lax.rem(chip + 1 + step, chips)

    offsets = [(dy, dx, dc) for dy in range(plane_y) for dx in range(chips) for dc in range(2)][1:]
    offsets.sort(key=lambda o: -2 * min(o[0], plane_y - o[0]) - 2 * min(o[1], chips - o[1]) - o[2])
    steps = range(len(offsets))

    def plane_id(step, back=1):
        dy, dx, dc = offsets[step]
        y = lax.rem(my_y + plane_y + back * dy, plane_y)
        there = lax.rem(chip + chips + back * dx, chips) * 2 + (1 - core if dc else core)
        return y * blk_size + there, {"blk": there, "rep": my_z * plane_y + y}

    def z_id(step):
        there = lax.rem(my_z + step, z_size)
        return there, {"blk": blk, "rep": there * plane_y + my_y}

    barrier = pltpu.get_barrier_semaphore()
    if reduce_in:
        for step in reversed(steps):
            pl.semaphore_signal(barrier, inc=1, device_id=plane_id(step)[1], device_id_type=MESH)
        for step in range(1, z_size):
            pl.semaphore_signal(barrier, inc=1, device_id=z_id(step)[1], device_id_type=MESH)
        greeted = plane - 1 + z_size - 1
    else:
        pl.semaphore_signal(barrier, inc=1, device_id={"blk": sib, "rep": rep}, device_id_type=MESH)
        for step in range(chips - 1):
            pl.semaphore_signal(
                barrier, inc=1, device_id={"blk": other_chip(step) * 2 + core, "rep": rep}, device_id_type=MESH)
        greeted = chips

    loads = [pltpu.make_async_copy(grad_ref, grad, in_sem.at[0]),
             pltpu.make_async_copy(weight_ref, weight, in_sem.at[1])]
    for t in range(rows_per):
        loads.append(pltpu.make_async_copy(tv_ref.at[t], tv.at[t, pl.ds(0, slots)], in_sem.at[2 + t]))
    my_rows = pl.ds(pl.multiple_of(core * nodes, nodes), nodes)
    sib_rows = pl.ds(pl.multiple_of((1 - core) * nodes, nodes), nodes)
    loads.append(pltpu.make_async_copy(feat_ref, feats.at[chip, my_rows], in_sem.at[2 + rows_per]))
    loads.append(pltpu.make_async_copy(count_hbm, count_ref, in_sem.at[3 + rows_per]))
    loads.append(pltpu.make_async_copy(cols_hbm, cols_ref, in_sem.at[4 + rows_per]))
    loads.append(pltpu.make_async_copy(mask_ref, mask, in_sem.at[5 + rows_per]))
    for i in [3 + rows_per, 4 + rows_per] + list(range(2, 2 + rows_per)) + [0, 2 + rows_per]:
        loads[i].start()
    pl.semaphore_wait(barrier, greeted)

    def x_copy(origin, device, piece):
        lanes = pl.ds(piece * half, half)
        return pltpu.make_async_remote_copy(
            src_ref=feat_ref.at[:, lanes], dst_ref=feats.at[origin, my_rows, lanes],
            send_sem=f_send.at[device // 2, piece], recv_sem=f_recv.at[0, origin, piece],
            device_id={"blk": device, "rep": rep}, device_id_type=MESH)

    def send_x(step, piece):
        return x_copy(chip, other_chip(step) * 2 + core, piece)

    def came_x(q, piece):
        return x_copy(q, q * 2 + core, piece)

    def sib_copy(q, rows, piece):
        lanes = pl.ds(piece * half, half)
        return pltpu.make_async_remote_copy(
            src_ref=feats.at[q, rows, lanes], dst_ref=feats.at[q, rows, lanes],
            send_sem=fwd_send.at[q, piece], recv_sem=f_recv.at[1, q, piece],
            device_id={"blk": sib, "rep": rep}, device_id_type=MESH)

    def pass_on(q, piece):
        return sib_copy(q, my_rows, piece)

    def passed(q, piece):
        return sib_copy(q, sib_rows, piece)

    for piece in range(2):
        each(chips - 1, lambda step: send_x(step, piece).start())
    loads[1].start()
    loads[5 + rows_per].start()
    loads[2 + rows_per].wait()
    for piece in range(2):
        pass_on(chip, piece).start()

    loads[3 + rows_per].wait()
    loads[4 + rows_per].wait()
    loads[0].wait()
    for t in range(rows_per):
        loads[2 + t].wait()
        tv[t, slots] = jnp.zeros((tile, tile), BF16)

    used = [[jnp.where(s < count_ref[t], cols_ref[t, s], -1) for s in range(slots)] for t in range(rows_per)]

    def block_of(q, c):
        member = q * 2 + c
        bands = []
        for r in range(rows_per):
            column = (member * rep_size + rep) * rows_per + r
            pieces = []
            for t in range(rows_per):
                slot = jnp.int32(slots)
                for s in range(slots):
                    slot = jnp.where(used[t][s] == column, jnp.int32(s), slot)
                pieces.append(tv[t, slot])
            bands.append(jnp.concatenate(pieces, axis=1))
        return jnp.concatenate(bands, axis=0)

    def one_copy(q):
        return pltpu.make_async_remote_copy(
            src_ref=one_send.at[q], dst_ref=one_recv.at[q],
            send_sem=one_ssem.at[q], recv_sem=one_rsem.at[q],
            device_id={"blk": sib, "rep": rep}, device_id_type=MESH)

    def two_copy(q, slot):
        return pltpu.make_async_remote_copy(
            src_ref=two_send.at[q], dst_ref=two_recv.at[slot],
            send_sem=two_ssem.at[q], recv_sem=two_rsem.at[slot],
            device_id={"blk": q * 2 + core, "rep": rep}, device_id_type=MESH)

    def for_sibling(step):
        q = other_chip(step)
        block = block_of(q, 1 - core)
        one_send[q] = dot(block, grad[...]).astype(BF16)
        one_copy(q).start()
        dense[q, sib_rows] = block

    def for_core(step):
        q = other_chip(step)
        block = block_of(q, core)
        own[q] = dot(block, grad[...])
        dense[q, my_rows] = block

    def pair(step):
        q = other_chip(step)
        one_copy(q).wait_recv()
        total = own[q] + one_recv[q].astype(F32)
        own[q] = total
        two_send[q] = total.astype(BF16)

    each(chips, for_sibling)
    each(chips, for_core)
    each(chips, pair)

    def arrive(piece):
        rows = pl.ds(piece * half, half)
        term[rows] = dot(feats[chip, my_rows, rows], two_send[chip], ((0,), (0,)))

        def from_chip(step):
            q = other_chip(step)
            came_x(q, piece).wait_recv()
            pass_on(q, piece).start()
            term[rows] += dot(feats[q, my_rows, rows], two_send[q], ((0,), (0,)))

        each(chips - 1, from_chip)

    def forward_own():
        for piece in range(2):
            passed(chip, piece).wait_recv()
        act[...] = dot(dense[chip], feats[chip], ((0,), (0,)))

    def forward_others():
        def from_chip(step):
            q = other_chip(step)
            for piece in range(2):
                passed(q, piece).wait_recv()
            act[...] += dot(dense[q], feats[q], ((0,), (0,)))

        each(chips - 1, from_chip)

    def activate():
        loads[1].wait()
        act_ref[...] = jnp.maximum(dot(act[...].astype(BF16), weight[...]), 0.0).astype(BF16)

    def columns():
        col[...] = own[chip]

        def from_chip(step):
            q = other_chip(step)
            two_copy(q, q).wait_recv()
            col[...] += two_recv[q].astype(F32)

        each(chips - 1, from_chip)
        high = col[...].astype(BF16)
        low = (col[...] - high.astype(F32)).astype(BF16)
        back = dot(high, weight[...], ((1,), (1,))) + dot(low, weight[...], ((1,), (1,)))
        loads[5 + rows_per].wait()
        col_ref[...] = (mask[...].astype(F32) * back).astype(BF16)

    def second(step):
        q = other_chip(step)
        two_copy(q, chip).start()

    def sent():
        for piece in range(2):
            each(chips - 1, lambda step: send_x(step, piece).wait_send())
            each(chips, lambda step: pass_on(other_chip(step), piece).wait_send())
        each(chips, lambda step: one_copy(other_chip(step)).wait_send())
        each(chips - 1, lambda step: two_copy(other_chip(step), chip).wait_send())

    if reduce_in:
        share = half // plane
        scale = 1.0 / math.sqrt(nodes * blk_size * rep_size)

        def rows_of(piece, owner):
            return pl.ds(pl.multiple_of(piece * half + owner * share, share), share)

        def rs_copy(piece, step):
            there, device = plane_id(step)
            return pltpu.make_async_remote_copy(
                src_ref=wg_part.at[rows_of(piece, there)], dst_ref=rs_recv.at[piece, step],
                send_sem=rs_ssem.at[piece, step], recv_sem=rs_rsem.at[piece, step],
                device_id=device, device_id_type=MESH)

        def z_copy(piece, step, slot):
            return pltpu.make_async_remote_copy(
                src_ref=z_buf.at[piece, my_z], dst_ref=z_buf.at[piece, slot],
                send_sem=z_ssem.at[piece, step - 1], recv_sem=z_rsem.at[piece, slot],
                device_id=z_id(step)[1], device_id_type=MESH)

        def ag_copy(piece, step, owner):
            rows = rows_of(piece, owner)
            return pltpu.make_async_remote_copy(
                src_ref=wg_full.at[rows], dst_ref=wg_full.at[rows],
                send_sem=ag_ssem.at[piece, step], recv_sem=ag_rsem.at[piece, step],
                device_id=plane_id(step)[1], device_id_type=MESH)

        for piece in range(2):
            arrive(piece)
            rows = pl.ds(piece * half, half)
            wg_part[rows] = term[rows].astype(BF16)
            for step in steps:
                rs_copy(piece, step).start()
        forward_own()
        for piece in range(2):
            total = term[rows_of(piece, place)]
            for step in steps:
                rs_copy(piece, step).wait_recv()
                total = total + rs_recv[piece, step].astype(F32)
            z_buf[piece, my_z] = total.astype(BF16)
            for step in range(1, z_size):
                z_copy(piece, step, my_z).start()
        each(chips - 1, second)
        forward_others()
        for piece in range(2):
            for step in range(1, z_size):
                z_copy(piece, step, z_id(step)[0]).wait_recv()
            total = z_buf[piece, 0].astype(F32)
            for z in range(1, z_size):
                total = total + z_buf[piece, z].astype(F32)
            wg_full[rows_of(piece, place)] = (total * scale).astype(BF16)
            for step in steps:
                ag_copy(piece, step, place).start()
            if piece == 0:
                activate()
        columns()
        sent()
        for piece in range(2):
            for step in steps:
                rs_copy(piece, step).wait_send()
                ag_copy(piece, step, place).wait_send()
            for step in range(1, z_size):
                z_copy(piece, step, my_z).wait_send()
        for piece in range(2):
            for step in steps:
                ag_copy(piece, step, plane_id(step, -1)[0]).wait_recv()
            rows = pl.ds(piece * half, half)
            wg_ref[rows] = wg_full[rows].astype(F32)
    else:
        for piece in range(2):
            arrive(piece)
        wg_ref[...] = term[...]
        each(chips - 1, second)
        forward_own()
        forward_others()
        activate()
        columns()
        sent()


def write_out(a_ref, b_ref, c_ref, a_out, b_out, c_out, sem):
    copies = [pltpu.make_async_copy(src, dst, sem.at[i])
              for i, (src, dst) in enumerate(((a_ref, a_out), (b_ref, b_out), (c_ref, c_out)))]
    for copy in copies:
        copy.start()
    for copy in copies:
        copy.wait()


def per_device(features, weight, tile_values, tile_count, tile_cols, out_grad, relu_mask):
    rows_per, slots, tile = tile_values.shape[:3]
    width = features.shape[2]
    nodes = rows_per * tile
    blk_size, rep_size = lax.axis_size("blk"), lax.axis_size("rep")
    chips = blk_size // 2
    plane_y = 2
    z_size = rep_size // plane_y
    plane = blk_size * plane_y
    reduce_in = width % (plane * 32) == 0 and z_size <= 8
    share = width // 2 // plane if reduce_in else 16
    block = (nodes, width)
    dma = pltpu.SemaphoreType.DMA
    vmem = pltpu.VMEM
    scratch = [
        pltpu.SMEM((rows_per,), jnp.int32),
        pltpu.SMEM((rows_per, slots), jnp.int32),
        vmem(block, jnp.int32),
        vmem((rows_per, slots + 1, tile, tile), BF16),
        vmem(block, BF16),
        vmem((width, width), BF16),
        vmem((chips, 2 * nodes, width), BF16),
        vmem((chips, 2 * nodes, nodes), BF16),
        vmem((chips,) + block, F32),
        vmem((chips,) + block, BF16),
        vmem((chips,) + block, BF16),
        vmem((chips,) + block, BF16),
        vmem((chips,) + block, BF16),
        vmem(block, F32),
        vmem(block, F32),
        vmem((width, width), F32),
        vmem((width, width), BF16),
        vmem((2, plane - 1, share, width), BF16),
        vmem((2, z_size, share, width), BF16),
        vmem((width, width), BF16),
        dma((6 + rows_per,)),
        dma((chips, 2)), dma((2, chips, 2)), dma((chips, 2)),
        dma((chips,)), dma((chips,)), dma((chips,)), dma((chips,)),
        dma((2, plane - 1)), dma((2, plane - 1)), dma((2, z_size)), dma((2, z_size)),
        dma((2, plane - 1)), dma((2, plane - 1)),
    ]
    hbm = pl.BlockSpec(memory_space=pltpu.HBM)
    whole = pl.BlockSpec(memory_space=pltpu.VMEM)
    dims = (blk_size, rep_size, rows_per, slots, tile, width, plane_y, reduce_in)
    results = pl.pallas_call(
        functools.partial(kernel, dims),
        out_shape=(
            jax.ShapeDtypeStruct(block, BF16),
            jax.ShapeDtypeStruct(block, BF16),
            jax.ShapeDtypeStruct((width, width), F32),
        ),
        in_specs=[hbm] * 7,
        out_specs=(whole, whole, whole),
        scratch_shapes=scratch,
        compiler_params=pltpu.CompilerParams(
            collective_id=0, has_side_effects=True, vmem_limit_bytes=32 * 1024 * 1024
        ),
        name="layer",
    )(*[pltpu.with_memory_space_constraint(x, pltpu.HBM) for x in (
        tile_count, tile_cols, features.reshape(block), tile_values, out_grad.reshape(block), weight,
        relu_mask.reshape(block))])
    activated, in_grad, weight_term = pl.pallas_call(
        write_out,
        out_shape=tuple(jax.ShapeDtypeStruct(r.shape, r.dtype) for r in results),
        in_specs=[whole] * 3,
        out_specs=(hbm, hbm, hbm),
        scratch_shapes=[dma((3,))],
        compiler_params=pltpu.CompilerParams(vmem_limit_bytes=4 * 1024 * 1024),
        name="write_out",
    )(*results)
    activated, in_grad = activated.reshape(features.shape), in_grad.reshape(features.shape)
    if not reduce_in:
        scale = 1.0 / math.sqrt(nodes * blk_size * rep_size)
        weight_term = lax.psum(weight_term, ("blk", "rep")) * scale
    return (activated, weight_term, in_grad)


def solution(mesh):
    placed = (
        P(("blk", "rep"), None, None),
        P(),
        P(("blk", "rep"), None, None, None),
        P(("blk", "rep")),
        P(("blk", "rep"), None),
        P(("blk", "rep"), None, None),
        P(("blk", "rep"), None, None),
    )
    return jax.shard_map(
        per_device,
        mesh=mesh,
        in_specs=placed,
        out_specs=(P(("blk", "rep"), None, None), P(), P(("blk", "rep"), None, None)),
        check_vma=False,
    )
```

```python
import functools
import math

import jax
import jax.numpy as jnp
from jax import lax
from jax.experimental import pallas as pl
from jax.experimental.pallas import tpu as pltpu
from jax.sharding import PartitionSpec as P

MESH = pl.DeviceIdType.MESH
BF16 = jnp.bfloat16
F32 = jnp.float32


def each(count, body):
    if count <= 2:
        for step in range(count):
            body(step)
    else:
        lax.fori_loop(0, count, lambda step, carry: (body(step), carry)[1], 0)


def dot(a, b, contract=((1,), (0,))):
    return lax.dot_general(a, b, (contract, ((), ())), preferred_element_type=F32)


def kernel(dims, *refs):
    blk_size, rep_size, rows_per, slots, tile, width, plane_y, reduce_in = dims
    (count_hbm, cols_hbm, feat_ref, tv_ref, grad_ref, weight_ref, mask_ref) = refs[:7]
    (act_ref, col_ref, wg_ref) = refs[7:10]
    (count_ref, cols_ref, mask, tv, grad, weight, arrived, feats, dense, own, one_send, one_recv, two_send, two_recv,
     act, col, term, wg_part, rs_recv, z_buf, wg_full,
     in_sem, f_send, f_recv, fwd_send, one_ssem, one_rsem, two_ssem, two_rsem,
     rs_ssem, rs_rsem, z_ssem, z_rsem, ag_ssem, ag_rsem) = refs[10:]
    nodes, half = rows_per * tile, width // 2
    chips = blk_size // 2
    z_size = rep_size // plane_y
    plane = blk_size * plane_y
    blk, rep = lax.axis_index("blk"), lax.axis_index("rep")
    chip, core = blk // 2, lax.rem(blk, 2)
    sib = chip * 2 + 1 - core
    my_y, my_z = lax.rem(rep, plane_y), rep // plane_y
    place = my_y * blk_size + blk

    def other_chip(step):
        return lax.rem(chip + 1 + step, chips)

    def plane_id(step):
        there = lax.rem(place + step, plane)
        return there, {"blk": lax.rem(there, blk_size), "rep": my_z * plane_y + there // blk_size}

    def z_id(step):
        there = lax.rem(my_z + step, z_size)
        return there, {"blk": blk, "rep": there * plane_y + my_y}

    barrier = pltpu.get_barrier_semaphore()
    if reduce_in:
        for step in sorted(range(1, plane), key=lambda s: min(s, plane - s)):
            pl.semaphore_signal(barrier, inc=1, device_id=plane_id(step)[1], device_id_type=MESH)
        for step in range(1, z_size):
            pl.semaphore_signal(barrier, inc=1, device_id=z_id(step)[1], device_id_type=MESH)
        greeted = plane - 1 + z_size - 1
    else:
        pl.semaphore_signal(barrier, inc=1, device_id={"blk": sib, "rep": rep}, device_id_type=MESH)
        for step in range(chips - 1):
            pl.semaphore_signal(
                barrier, inc=1, device_id={"blk": other_chip(step) * 2 + core, "rep": rep}, device_id_type=MESH)
        greeted = chips

    loads = [pltpu.make_async_copy(grad_ref, grad, in_sem.at[0]),
             pltpu.make_async_copy(weight_ref, weight, in_sem.at[1])]
    for t in range(rows_per):
        loads.append(pltpu.make_async_copy(tv_ref.at[t], tv.at[t, pl.ds(0, slots)], in_sem.at[2 + t]))
    my_rows = pl.ds(pl.multiple_of(core * nodes, nodes), nodes)
    sib_rows = pl.ds(pl.multiple_of((1 - core) * nodes, nodes), nodes)
    loads.append(pltpu.make_async_copy(feat_ref, arrived.at[chip], in_sem.at[2 + rows_per]))
    loads.append(pltpu.make_async_copy(count_hbm, count_ref, in_sem.at[3 + rows_per]))
    loads.append(pltpu.make_async_copy(cols_hbm, cols_ref, in_sem.at[4 + rows_per]))
    loads.append(pltpu.make_async_copy(mask_ref, mask, in_sem.at[5 + rows_per]))
    for i in [3 + rows_per, 4 + rows_per] + list(range(2, 2 + rows_per)) + [0, 2 + rows_per]:
        loads[i].start()
    pl.semaphore_wait(barrier, greeted)

    def x_copy(origin, device, piece):
        lanes = pl.ds(piece * half, half)
        return pltpu.make_async_remote_copy(
            src_ref=feat_ref.at[:, lanes], dst_ref=arrived.at[origin, :, lanes],
            send_sem=f_send.at[device // 2, piece], recv_sem=f_recv.at[0, origin, piece],
            device_id={"blk": device, "rep": rep}, device_id_type=MESH)

    def send_x(step, piece):
        return x_copy(chip, other_chip(step) * 2 + core, piece)

    def came_x(q, piece):
        return x_copy(q, q * 2 + core, piece)

    def sib_copy(q, side, piece):
        rows = pl.ds(piece * half, half)
        return pltpu.make_async_remote_copy(
            src_ref=feats.at[q, rows, side], dst_ref=feats.at[q, rows, side],
            send_sem=fwd_send.at[q, piece], recv_sem=f_recv.at[1, q, piece],
            device_id={"blk": sib, "rep": rep}, device_id_type=MESH)

    def turn(q, piece):
        lanes = pl.ds(piece * half, half)
        feats[q, lanes, my_rows] = arrived[q, :, lanes].T
        pass_on(q, piece).start()

    def pass_on(q, piece):
        return sib_copy(q, my_rows, piece)

    def passed(q, piece):
        return sib_copy(q, sib_rows, piece)

    for piece in range(2):
        each(chips - 1, lambda step: send_x(step, piece).start())
    loads[1].start()
    loads[5 + rows_per].start()

    loads[3 + rows_per].wait()
    loads[4 + rows_per].wait()
    loads[0].wait()
    for t in range(rows_per):
        loads[2 + t].wait()
        tv[t, slots] = jnp.zeros((tile, tile), BF16)

    used = [[jnp.where(s < count_ref[t], cols_ref[t, s], -1) for s in range(slots)] for t in range(rows_per)]

    def block_of(q, c):
        member = q * 2 + c
        bands = []
        for r in range(rows_per):
            column = (member * rep_size + rep) * rows_per + r
            pieces = []
            for t in range(rows_per):
                slot = jnp.int32(slots)
                for s in range(slots):
                    slot = jnp.where(used[t][s] == column, jnp.int32(s), slot)
                pieces.append(tv[t, slot])
            bands.append(jnp.concatenate(pieces, axis=1))
        return jnp.concatenate(bands, axis=0)

    def one_copy(q):
        return pltpu.make_async_remote_copy(
            src_ref=one_send.at[q], dst_ref=one_recv.at[q],
            send_sem=one_ssem.at[q], recv_sem=one_rsem.at[q],
            device_id={"blk": sib, "rep": rep}, device_id_type=MESH)

    def two_copy(q, slot):
        return pltpu.make_async_remote_copy(
            src_ref=two_send.at[q], dst_ref=two_recv.at[slot],
            send_sem=two_ssem.at[q], recv_sem=two_rsem.at[slot],
            device_id={"blk": q * 2 + core, "rep": rep}, device_id_type=MESH)

    def for_sibling(step):
        q = other_chip(step)
        block = block_of(q, 1 - core)
        one_send[q] = dot(block, grad[...]).astype(BF16)
        one_copy(q).start()
        dense[q, sib_rows] = block

    def for_core(step):
        q = other_chip(step)
        block = block_of(q, core)
        own[q] = dot(block, grad[...])
        dense[q, my_rows] = block

    def pair(step):
        q = other_chip(step)
        one_copy(q).wait_recv()
        total = own[q] + one_recv[q].astype(F32)
        own[q] = total
        two_send[q] = total.astype(BF16)

    each(chips, for_sibling)
    each(chips, for_core)
    loads[2 + rows_per].wait()
    for piece in range(2):
        turn(chip, piece)
    each(chips, pair)

    def arrive(piece):
        rows = pl.ds(piece * half, half)
        term[rows] = dot(feats[chip, rows, my_rows], two_send[chip])

        def from_chip(step):
            q = other_chip(step)
            came_x(q, piece).wait_recv()
            turn(q, piece)
            term[rows] += dot(feats[q, rows, my_rows], two_send[q])

        each(chips - 1, from_chip)

    def forward():
        for piece in range(2):
            passed(chip, piece).wait_recv()
        act[...] = dot(feats[chip], dense[chip])

        def from_chip(step):
            q = other_chip(step)
            for piece in range(2):
                passed(q, piece).wait_recv()
            act[...] += dot(feats[q], dense[q])

        each(chips - 1, from_chip)

    def activate():
        loads[1].wait()
        act_ref[...] = jnp.maximum(dot(act[...].astype(BF16), weight[...], ((0,), (0,))), 0.0).astype(BF16)

    def columns():
        col[...] = own[chip]

        def from_chip(step):
            q = other_chip(step)
            two_copy(q, q).wait_recv()
            col[...] += two_recv[q].astype(F32)

        each(chips - 1, from_chip)
        high = col[...].astype(BF16)
        low = (col[...] - high.astype(F32)).astype(BF16)
        back = dot(high, weight[...], ((1,), (1,))) + dot(low, weight[...], ((1,), (1,)))
        loads[5 + rows_per].wait()
        col_ref[...] = (mask[...].astype(F32) * back).astype(BF16)

    def second(step):
        q = other_chip(step)
        two_copy(q, chip).start()

    def sent():
        for piece in range(2):
            each(chips - 1, lambda step: send_x(step, piece).wait_send())
            each(chips, lambda step: pass_on(other_chip(step), piece).wait_send())
        each(chips, lambda step: one_copy(other_chip(step)).wait_send())
        each(chips - 1, lambda step: two_copy(other_chip(step), chip).wait_send())

    if reduce_in:
        share = half // plane
        scale = 1.0 / math.sqrt(nodes * blk_size * rep_size)

        def rows_of(piece, owner):
            return pl.ds(pl.multiple_of(piece * half + owner * share, share), share)

        def rs_copy(piece, step):
            there, device = plane_id(step)
            return pltpu.make_async_remote_copy(
                src_ref=wg_part.at[rows_of(piece, there)], dst_ref=rs_recv.at[piece, step - 1],
                send_sem=rs_ssem.at[piece, step - 1], recv_sem=rs_rsem.at[piece, step - 1],
                device_id=device, device_id_type=MESH)

        def z_copy(piece, step, slot):
            return pltpu.make_async_remote_copy(
                src_ref=z_buf.at[piece, my_z], dst_ref=z_buf.at[piece, slot],
                send_sem=z_ssem.at[piece, step - 1], recv_sem=z_rsem.at[piece, slot],
                device_id=z_id(step)[1], device_id_type=MESH)

        def ag_copy(piece, step, owner):
            rows = rows_of(piece, owner)
            return pltpu.make_async_remote_copy(
                src_ref=wg_full.at[rows], dst_ref=wg_full.at[rows],
                send_sem=ag_ssem.at[piece, step - 1], recv_sem=ag_rsem.at[piece, step - 1],
                device_id=plane_id(step)[1], device_id_type=MESH)

        for piece in range(2):
            arrive(piece)
            rows = pl.ds(piece * half, half)
            wg_part[rows] = term[rows].astype(BF16)
            for step in range(1, plane):
                rs_copy(piece, step).start()
        for piece in range(2):
            total = term[rows_of(piece, place)]
            for step in range(1, plane):
                rs_copy(piece, step).wait_recv()
                total = total + rs_recv[piece, step - 1].astype(F32)
            z_buf[piece, my_z] = total.astype(BF16)
            for step in range(1, z_size):
                z_copy(piece, step, my_z).start()
        each(chips - 1, second)
        forward()
        for piece in range(2):
            for step in range(1, z_size):
                z_copy(piece, step, z_id(step)[0]).wait_recv()
            total = z_buf[piece, 0].astype(F32)
            for z in range(1, z_size):
                total = total + z_buf[piece, z].astype(F32)
            wg_full[rows_of(piece, place)] = (total * scale).astype(BF16)
            for step in range(1, plane):
                ag_copy(piece, step, place).start()
            if piece == 0:
                activate()
        columns()
        sent()
        for piece in range(2):
            for step in range(1, plane):
                rs_copy(piece, step).wait_send()
                ag_copy(piece, step, place).wait_send()
            for step in range(1, z_size):
                z_copy(piece, step, my_z).wait_send()
        for piece in range(2):
            for step in range(1, plane):
                ag_copy(piece, step, lax.rem(place + plane - step, plane)).wait_recv()
            rows = pl.ds(piece * half, half)
            wg_ref[rows] = wg_full[rows].astype(F32)
    else:
        for piece in range(2):
            arrive(piece)
        wg_ref[...] = term[...]
        each(chips - 1, second)
        forward()
        activate()
        columns()
        sent()


def write_out(a_ref, b_ref, c_ref, a_out, b_out, c_out, sem):
    copies = [pltpu.make_async_copy(src, dst, sem.at[i])
              for i, (src, dst) in enumerate(((a_ref, a_out), (b_ref, b_out), (c_ref, c_out)))]
    for copy in copies:
        copy.start()
    for copy in copies:
        copy.wait()


def per_device(features, weight, tile_values, tile_count, tile_cols, out_grad, relu_mask):
    rows_per, slots, tile = tile_values.shape[:3]
    width = features.shape[2]
    nodes = rows_per * tile
    blk_size, rep_size = lax.axis_size("blk"), lax.axis_size("rep")
    chips = blk_size // 2
    plane_y = 2
    z_size = rep_size // plane_y
    plane = blk_size * plane_y
    reduce_in = width % (plane * 32) == 0 and z_size <= 8
    share = width // 2 // plane if reduce_in else 16
    block = (nodes, width)
    dma = pltpu.SemaphoreType.DMA
    vmem = pltpu.VMEM
    scratch = [
        pltpu.SMEM((rows_per,), jnp.int32),
        pltpu.SMEM((rows_per, slots), jnp.int32),
        vmem(block, jnp.int32),
        vmem((rows_per, slots + 1, tile, tile), BF16),
        vmem(block, BF16),
        vmem((width, width), BF16),
        vmem((chips,) + block, BF16),
        vmem((chips, width, 2 * nodes), BF16),
        vmem((chips, 2 * nodes, nodes), BF16),
        vmem((chips,) + block, F32),
        vmem((chips,) + block, BF16),
        vmem((chips,) + block, BF16),
        vmem((chips,) + block, BF16),
        vmem((chips,) + block, BF16),
        vmem((width, nodes), F32),
        vmem(block, F32),
        vmem((width, width), F32),
        vmem((width, width), BF16),
        vmem((2, plane - 1, share, width), BF16),
        vmem((2, z_size, share, width), BF16),
        vmem((width, width), BF16),
        dma((6 + rows_per,)),
        dma((chips, 2)), dma((2, chips, 2)), dma((chips, 2)),
        dma((chips,)), dma((chips,)), dma((chips,)), dma((chips,)),
        dma((2, plane - 1)), dma((2, plane - 1)), dma((2, z_size)), dma((2, z_size)),
        dma((2, plane - 1)), dma((2, plane - 1)),
    ]
    hbm = pl.BlockSpec(memory_space=pltpu.HBM)
    whole = pl.BlockSpec(memory_space=pltpu.VMEM)
    dims = (blk_size, rep_size, rows_per, slots, tile, width, plane_y, reduce_in)
    results = pl.pallas_call(
        functools.partial(kernel, dims),
        out_shape=(
            jax.ShapeDtypeStruct(block, BF16),
            jax.ShapeDtypeStruct(block, BF16),
            jax.ShapeDtypeStruct((width, width), F32),
        ),
        in_specs=[hbm] * 7,
        out_specs=(whole, whole, whole),
        scratch_shapes=scratch,
        compiler_params=pltpu.CompilerParams(
            collective_id=0, has_side_effects=True, vmem_limit_bytes=32 * 1024 * 1024
        ),
        name="layer",
    )(*[pltpu.with_memory_space_constraint(x, pltpu.HBM) for x in (
        tile_count, tile_cols, features.reshape(block), tile_values, out_grad.reshape(block), weight,
        relu_mask.reshape(block))])
    activated, in_grad, weight_term = pl.pallas_call(
        write_out,
        out_shape=tuple(jax.ShapeDtypeStruct(r.shape, r.dtype) for r in results),
        in_specs=[whole] * 3,
        out_specs=(hbm, hbm, hbm),
        scratch_shapes=[dma((3,))],
        compiler_params=pltpu.CompilerParams(vmem_limit_bytes=4 * 1024 * 1024),
        name="write_out",
    )(*results)
    activated, in_grad = activated.reshape(features.shape), in_grad.reshape(features.shape)
    if not reduce_in:
        scale = 1.0 / math.sqrt(nodes * blk_size * rep_size)
        weight_term = lax.psum(weight_term, ("blk", "rep")) * scale
    return (activated, weight_term, in_grad)


def solution(mesh):
    placed = (
        P(("blk", "rep"), None, None),
        P(),
        P(("blk", "rep"), None, None, None),
        P(("blk", "rep")),
        P(("blk", "rep"), None),
        P(("blk", "rep"), None, None),
        P(("blk", "rep"), None, None),
    )
    return jax.shard_map(
        per_device,
        mesh=mesh,
        in_specs=placed,
        out_specs=(P(("blk", "rep"), None, None), P(), P(("blk", "rep"), None, None)),
        check_vma=False,
    )
```

```python
import functools
import math

import jax
import jax.numpy as jnp
from jax import lax
from jax.experimental import pallas as pl
from jax.experimental.pallas import tpu as pltpu
from jax.sharding import PartitionSpec as P

MESH = pl.DeviceIdType.MESH
BF16 = jnp.bfloat16
F32 = jnp.float32


def each(count, body):
    if count <= 2:
        for step in range(count):
            body(step)
    else:
        lax.fori_loop(0, count, lambda step, carry: (body(step), carry)[1], 0)


def dot(a, b, contract=((1,), (0,))):
    return lax.dot_general(a, b, (contract, ((), ())), preferred_element_type=F32)


def kernel(dims, *refs):
    blk_size, rep_size, rows_per, slots, tile, width, plane_y, reduce_in = dims
    (count_hbm, cols_hbm, feat_ref, tv_ref, grad_ref, weight_ref, mask_ref) = refs[:7]
    (act_ref, col_ref, wg_ref) = refs[7:10]
    (count_ref, cols_ref, mask, tv, grad, weight, arrived, feats, dense, own, one_send, one_recv, two_send, two_recv,
     act, col, term, wg_part, rs_recv, z_buf, wg_full,
     in_sem, f_send, f_recv, fwd_send, one_ssem, one_rsem, two_ssem, two_rsem,
     rs_ssem, rs_rsem, z_ssem, z_rsem, ag_ssem, ag_rsem) = refs[10:]
    nodes, half = rows_per * tile, width // 2
    chips = blk_size // 2
    z_size = rep_size // plane_y
    plane = blk_size * plane_y
    blk, rep = lax.axis_index("blk"), lax.axis_index("rep")
    chip, core = blk // 2, lax.rem(blk, 2)
    sib = chip * 2 + 1 - core
    my_y, my_z = lax.rem(rep, plane_y), rep // plane_y
    place = my_y * blk_size + blk

    def other_chip(step):
        return lax.rem(chip + 1 + step, chips)

    def plane_id(step):
        there = lax.rem(place + step, plane)
        return there, {"blk": lax.rem(there, blk_size), "rep": my_z * plane_y + there // blk_size}

    def z_id(step):
        there = lax.rem(my_z + step, z_size)
        return there, {"blk": blk, "rep": there * plane_y + my_y}

    barrier = pltpu.get_barrier_semaphore()
    if reduce_in:
        for step in range(z_size - 1, 0, -1):
            pl.semaphore_signal(barrier, inc=1, device_id=z_id(step)[1], device_id_type=MESH)
        for step in sorted(range(1, plane), key=lambda s: -min(s, plane - s)):
            pl.semaphore_signal(barrier, inc=1, device_id=plane_id(step)[1], device_id_type=MESH)
        greeted = plane - 1 + z_size - 1
    else:
        pl.semaphore_signal(barrier, inc=1, device_id={"blk": sib, "rep": rep}, device_id_type=MESH)
        for step in range(chips - 1):
            pl.semaphore_signal(
                barrier, inc=1, device_id={"blk": other_chip(step) * 2 + core, "rep": rep}, device_id_type=MESH)
        greeted = chips

    loads = [pltpu.make_async_copy(grad_ref, grad, in_sem.at[0]),
             pltpu.make_async_copy(weight_ref, weight, in_sem.at[1])]
    for t in range(rows_per):
        loads.append(pltpu.make_async_copy(tv_ref.at[t], tv.at[t, pl.ds(0, slots)], in_sem.at[2 + t]))
    my_rows = pl.ds(pl.multiple_of(core * nodes, nodes), nodes)
    sib_rows = pl.ds(pl.multiple_of((1 - core) * nodes, nodes), nodes)
    loads.append(pltpu.make_async_copy(feat_ref, arrived.at[chip], in_sem.at[2 + rows_per]))
    loads.append(pltpu.make_async_copy(count_hbm, count_ref, in_sem.at[3 + rows_per]))
    loads.append(pltpu.make_async_copy(cols_hbm, cols_ref, in_sem.at[4 + rows_per]))
    loads.append(pltpu.make_async_copy(mask_ref, mask, in_sem.at[5 + rows_per]))
    for i in [3 + rows_per, 4 + rows_per] + list(range(2, 2 + rows_per)) + [0, 2 + rows_per]:
        loads[i].start()
    pl.semaphore_wait(barrier, greeted)

    def x_copy(origin, device, piece):
        lanes = pl.ds(piece * half, half)
        return pltpu.make_async_remote_copy(
            src_ref=feat_ref.at[:, lanes], dst_ref=arrived.at[origin, :, lanes],
            send_sem=f_send.at[device // 2, piece], recv_sem=f_recv.at[0, origin, piece],
            device_id={"blk": device, "rep": rep}, device_id_type=MESH)

    def send_x(step, piece):
        return x_copy(chip, other_chip(step) * 2 + core, piece)

    def came_x(q, piece):
        return x_copy(q, q * 2 + core, piece)

    def sib_copy(q, side, piece):
        rows = pl.ds(piece * half, half)
        return pltpu.make_async_remote_copy(
            src_ref=feats.at[q, rows, side], dst_ref=feats.at[q, rows, side],
            send_sem=fwd_send.at[q, piece], recv_sem=f_recv.at[1, q, piece],
            device_id={"blk": sib, "rep": rep}, device_id_type=MESH)

    def turn(q, piece):
        lanes = pl.ds(piece * half, half)
        feats[q, lanes, my_rows] = arrived[q, :, lanes].T
        pass_on(q, piece).start()

    def pass_on(q, piece):
        return sib_copy(q, my_rows, piece)

    def passed(q, piece):
        return sib_copy(q, sib_rows, piece)

    for piece in range(2):
        each(chips - 1, lambda step: send_x(step, piece).start())
    loads[1].start()
    loads[5 + rows_per].start()

    loads[3 + rows_per].wait()
    loads[4 + rows_per].wait()
    loads[0].wait()
    for t in range(rows_per):
        loads[2 + t].wait()
        tv[t, slots] = jnp.zeros((tile, tile), BF16)

    used = [[jnp.where(s < count_ref[t], cols_ref[t, s], -1) for s in range(slots)] for t in range(rows_per)]

    def block_of(q, c):
        member = q * 2 + c
        bands = []
        for r in range(rows_per):
            column = (member * rep_size + rep) * rows_per + r
            pieces = []
            for t in range(rows_per):
                slot = jnp.int32(slots)
                for s in range(slots):
                    slot = jnp.where(used[t][s] == column, jnp.int32(s), slot)
                pieces.append(tv[t, slot])
            bands.append(jnp.concatenate(pieces, axis=1))
        return jnp.concatenate(bands, axis=0)

    def one_copy(q):
        return pltpu.make_async_remote_copy(
            src_ref=one_send.at[q], dst_ref=one_recv.at[q],
            send_sem=one_ssem.at[q], recv_sem=one_rsem.at[q],
            device_id={"blk": sib, "rep": rep}, device_id_type=MESH)

    def two_copy(q, slot):
        return pltpu.make_async_remote_copy(
            src_ref=two_send.at[q], dst_ref=two_recv.at[slot],
            send_sem=two_ssem.at[q], recv_sem=two_rsem.at[slot],
            device_id={"blk": q * 2 + core, "rep": rep}, device_id_type=MESH)

    def for_sibling(step):
        q = other_chip(step)
        block = block_of(q, 1 - core)
        one_send[q] = dot(block, grad[...]).astype(BF16)
        one_copy(q).start()
        dense[q, sib_rows] = block

    def for_core(step):
        q = other_chip(step)
        block = block_of(q, core)
        own[q] = dot(block, grad[...])
        dense[q, my_rows] = block

    def pair(step):
        q = other_chip(step)
        one_copy(q).wait_recv()
        total = own[q] + one_recv[q].astype(F32)
        own[q] = total
        two_send[q] = total.astype(BF16)

    each(chips, for_sibling)
    each(chips, for_core)
    loads[2 + rows_per].wait()
    for piece in range(2):
        turn(chip, piece)
    each(chips, pair)

    def arrive(piece):
        rows = pl.ds(piece * half, half)
        term[rows] = dot(feats[chip, rows, my_rows], two_send[chip])

        def from_chip(step):
            q = other_chip(step)
            came_x(q, piece).wait_recv()
            turn(q, piece)
            term[rows] += dot(feats[q, rows, my_rows], two_send[q])

        each(chips - 1, from_chip)

    def forward():
        for piece in range(2):
            passed(chip, piece).wait_recv()
        act[...] = dot(feats[chip], dense[chip])

        def from_chip(step):
            q = other_chip(step)
            for piece in range(2):
                passed(q, piece).wait_recv()
            act[...] += dot(feats[q], dense[q])

        each(chips - 1, from_chip)

    def activate():
        loads[1].wait()
        act_ref[...] = jnp.maximum(dot(act[...].astype(BF16), weight[...], ((0,), (0,))), 0.0).astype(BF16)

    def columns():
        col[...] = own[chip]

        def from_chip(step):
            q = other_chip(step)
            two_copy(q, q).wait_recv()
            col[...] += two_recv[q].astype(F32)

        each(chips - 1, from_chip)
        high = col[...].astype(BF16)
        low = (col[...] - high.astype(F32)).astype(BF16)
        back = dot(high, weight[...], ((1,), (1,))) + dot(low, weight[...], ((1,), (1,)))
        loads[5 + rows_per].wait()
        col_ref[...] = (mask[...].astype(F32) * back).astype(BF16)

    def second(step):
        q = other_chip(step)
        two_copy(q, chip).start()

    def sent():
        for piece in range(2):
            each(chips - 1, lambda step: send_x(step, piece).wait_send())
            each(chips, lambda step: pass_on(other_chip(step), piece).wait_send())
        each(chips, lambda step: one_copy(other_chip(step)).wait_send())
        each(chips - 1, lambda step: two_copy(other_chip(step), chip).wait_send())

    if reduce_in:
        share = half // plane
        scale = 1.0 / math.sqrt(nodes * blk_size * rep_size)

        def rows_of(piece, owner):
            return pl.ds(pl.multiple_of(piece * half + owner * share, share), share)

        def rs_copy(piece, step):
            there, device = plane_id(step)
            return pltpu.make_async_remote_copy(
                src_ref=wg_part.at[rows_of(piece, there)], dst_ref=rs_recv.at[piece, step - 1],
                send_sem=rs_ssem.at[piece, step - 1], recv_sem=rs_rsem.at[piece, step - 1],
                device_id=device, device_id_type=MESH)

        def z_copy(piece, step, slot):
            return pltpu.make_async_remote_copy(
                src_ref=z_buf.at[piece, my_z], dst_ref=z_buf.at[piece, slot],
                send_sem=z_ssem.at[piece, step - 1], recv_sem=z_rsem.at[piece, slot],
                device_id=z_id(step)[1], device_id_type=MESH)

        def ag_copy(piece, step, owner):
            rows = rows_of(piece, owner)
            return pltpu.make_async_remote_copy(
                src_ref=wg_full.at[rows], dst_ref=wg_full.at[rows],
                send_sem=ag_ssem.at[piece, step - 1], recv_sem=ag_rsem.at[piece, step - 1],
                device_id=plane_id(step)[1], device_id_type=MESH)

        for piece in range(2):
            arrive(piece)
            rows = pl.ds(piece * half, half)
            wg_part[rows] = term[rows].astype(BF16)
            for step in range(1, plane):
                rs_copy(piece, step).start()
        for piece in range(2):
            total = term[rows_of(piece, place)]
            for step in range(1, plane):
                rs_copy(piece, step).wait_recv()
                total = total + rs_recv[piece, step - 1].astype(F32)
            z_buf[piece, my_z] = total.astype(BF16)
            for step in range(1, z_size):
                z_copy(piece, step, my_z).start()
        each(chips - 1, second)
        forward()
        for piece in range(2):
            for step in range(1, z_size):
                z_copy(piece, step, z_id(step)[0]).wait_recv()
            total = z_buf[piece, 0].astype(F32)
            for z in range(1, z_size):
                total = total + z_buf[piece, z].astype(F32)
            wg_full[rows_of(piece, place)] = (total * scale).astype(BF16)
            for step in range(1, plane):
                ag_copy(piece, step, place).start()
            if piece == 0:
                activate()
        columns()
        sent()
        for piece in range(2):
            for step in range(1, plane):
                rs_copy(piece, step).wait_send()
                ag_copy(piece, step, place).wait_send()
            for step in range(1, z_size):
                z_copy(piece, step, my_z).wait_send()
        for piece in range(2):
            for step in range(1, plane):
                ag_copy(piece, step, lax.rem(place + plane - step, plane)).wait_recv()
            rows = pl.ds(piece * half, half)
            wg_ref[rows] = wg_full[rows].astype(F32)
    else:
        for piece in range(2):
            arrive(piece)
        wg_ref[...] = term[...]
        each(chips - 1, second)
        forward()
        activate()
        columns()
        sent()


def write_out(a_ref, b_ref, c_ref, a_out, b_out, c_out, sem):
    copies = [pltpu.make_async_copy(src, dst, sem.at[i])
              for i, (src, dst) in enumerate(((a_ref, a_out), (b_ref, b_out), (c_ref, c_out)))]
    for copy in copies:
        copy.start()
    for copy in copies:
        copy.wait()


def per_device(features, weight, tile_values, tile_count, tile_cols, out_grad, relu_mask):
    rows_per, slots, tile = tile_values.shape[:3]
    width = features.shape[2]
    nodes = rows_per * tile
    blk_size, rep_size = lax.axis_size("blk"), lax.axis_size("rep")
    chips = blk_size // 2
    plane_y = 2
    z_size = rep_size // plane_y
    plane = blk_size * plane_y
    reduce_in = width % (plane * 32) == 0 and z_size <= 8
    share = width // 2 // plane if reduce_in else 16
    block = (nodes, width)
    dma = pltpu.SemaphoreType.DMA
    vmem = pltpu.VMEM
    scratch = [
        pltpu.SMEM((rows_per,), jnp.int32),
        pltpu.SMEM((rows_per, slots), jnp.int32),
        vmem(block, jnp.int32),
        vmem((rows_per, slots + 1, tile, tile), BF16),
        vmem(block, BF16),
        vmem((width, width), BF16),
        vmem((chips,) + block, BF16),
        vmem((chips, width, 2 * nodes), BF16),
        vmem((chips, 2 * nodes, nodes), BF16),
        vmem((chips,) + block, F32),
        vmem((chips,) + block, BF16),
        vmem((chips,) + block, BF16),
        vmem((chips,) + block, BF16),
        vmem((chips,) + block, BF16),
        vmem((width, nodes), F32),
        vmem(block, F32),
        vmem((width, width), F32),
        vmem((width, width), BF16),
        vmem((2, plane - 1, share, width), BF16),
        vmem((2, z_size, share, width), BF16),
        vmem((width, width), BF16),
        dma((6 + rows_per,)),
        dma((chips, 2)), dma((2, chips, 2)), dma((chips, 2)),
        dma((chips,)), dma((chips,)), dma((chips,)), dma((chips,)),
        dma((2, plane - 1)), dma((2, plane - 1)), dma((2, z_size)), dma((2, z_size)),
        dma((2, plane - 1)), dma((2, plane - 1)),
    ]
    hbm = pl.BlockSpec(memory_space=pltpu.HBM)
    whole = pl.BlockSpec(memory_space=pltpu.VMEM)
    dims = (blk_size, rep_size, rows_per, slots, tile, width, plane_y, reduce_in)
    results = pl.pallas_call(
        functools.partial(kernel, dims),
        out_shape=(
            jax.ShapeDtypeStruct(block, BF16),
            jax.ShapeDtypeStruct(block, BF16),
            jax.ShapeDtypeStruct((width, width), F32),
        ),
        in_specs=[hbm] * 7,
        out_specs=(whole, whole, whole),
        scratch_shapes=scratch,
        compiler_params=pltpu.CompilerParams(
            collective_id=0, has_side_effects=True, vmem_limit_bytes=32 * 1024 * 1024
        ),
        name="layer",
    )(*[pltpu.with_memory_space_constraint(x, pltpu.HBM) for x in (
        tile_count, tile_cols, features.reshape(block), tile_values, out_grad.reshape(block), weight,
        relu_mask.reshape(block))])
    activated, in_grad, weight_term = pl.pallas_call(
        write_out,
        out_shape=tuple(jax.ShapeDtypeStruct(r.shape, r.dtype) for r in results),
        in_specs=[whole] * 3,
        out_specs=(hbm, hbm, hbm),
        scratch_shapes=[dma((3,))],
        compiler_params=pltpu.CompilerParams(vmem_limit_bytes=4 * 1024 * 1024),
        name="write_out",
    )(*results)
    activated, in_grad = activated.reshape(features.shape), in_grad.reshape(features.shape)
    if not reduce_in:
        scale = 1.0 / math.sqrt(nodes * blk_size * rep_size)
        weight_term = lax.psum(weight_term, ("blk", "rep")) * scale
    return (activated, weight_term, in_grad)


def solution(mesh):
    placed = (
        P(("blk", "rep"), None, None),
        P(),
        P(("blk", "rep"), None, None, None),
        P(("blk", "rep")),
        P(("blk", "rep"), None),
        P(("blk", "rep"), None, None),
        P(("blk", "rep"), None, None),
    )
    return jax.shard_map(
        per_device,
        mesh=mesh,
        in_specs=placed,
        out_specs=(P(("blk", "rep"), None, None), P(), P(("blk", "rep"), None, None)),
        check_vma=False,
    )
```
